32 devices in a mesh: sec: 2 (over x), gx: 4 (over z), az: 4 (over y, core).
Axes of the slice: x: 2, y: 2, z: 4, core: 2. Of those that a mesh axis runs over, the one named last changes fastest.
Arguments:
- les_velocity: float32 [3, 8, 64, 1024], P(None, None, 'az', ('sec', 'gx')), may hold values from -6 to 6
- les_metric: float32 [3, 8, 64, 1024], P(None, None, 'az', ('sec', 'gx')), may hold values from 0.5 to 1.5
- caa_state: float32 [4, 8, 64, 1024], P(None, None, 'az', ('sec', 'gx')), may hold values from -6 to 6
- caa_metric: float32 [3, 8, 64, 1024], P(None, None, 'az', ('sec', 'gx')), may hold values from 0.5 to 1.5
- intersection_refs: int32 [128, 4], P(('sec', 'gx')), may hold values from 0 to 7, as said below
- offsets: int32 [128], P(('sec', 'gx')), may hold values from 0 to 8
- send_list: int32 [8, 4, 8], replicated, may hold values from -1 to 15, as said below
Outputs:
- les_out: float32 [3, 8, 64, 1024], P(None, None, 'az', ('sec', 'gx'))
- caa_out: float32 [4, 8, 64, 1024], P(None, None, 'az', ('sec', 'gx'))
The draws below stay inside these ranges and needn't reach their ends.
Inputs may be any that keep to these rules, and one draw needn't show every extreme that they name: `intersection_refs`: row j belongs to slab r = j // 16; columns 0 and 2 are slabs of r's section (0 to 3), columns 1 and 3 slots (0 to 7). Among the 32 pairs of one slab no (slab, slot) pair repeats, at most 8 name one slab and exactly 8 name some slab, the slots towards one slab are filled from 0 upward, and send_list holds a block (not -1) at every named pair. send_list[s, d, c] is a block of slab s (0 to 15) for slot c of slab d of the same section, and -1 exactly where no row of slab d names (s, c).
All inputs are finite; a program needn't handle non-finite values.
Results may differ from the reference program's by a relative error of at most 0.00081.
Values may be sent and summed in bfloat16 or wider, within the bound.
A program may use at most 64 MiB of HBM per device.

```python
import math
import jax
import jax.numpy as jnp
import numpy as np
from jax import lax

NR = 8
B = 16
LES_STEPS = 2
CAA_SUB = 4
CAP = 8
NA = 64
NS = 1024
SLOTS = 128
N_SEC = 2
N_GX = 4


def intersection_tables(key):
    base_key = jax.random.fold_in(key, 7177)
    row_count = N_SEC * N_GX
    row_keys = jax.random.split(base_key, row_count)

    def one_row(row_key):
        first_key, second_key, third_key, fourth_key = jax.random.split(row_key, 4)
        forced = jax.random.randint(first_key, (), 0, N_GX).astype(jnp.int32)
        others = jnp.arange(N_GX - 1, dtype=jnp.int32)
        others = jnp.where(others >= forced, others + 1, others)
        candidates = jax.random.permutation(second_key, jnp.repeat(others, CAP))
        chosen = jnp.concatenate([jnp.full((CAP,), forced, jnp.int32), candidates])[:2 * B]
        chosen = jax.random.permutation(third_key, chosen)
        earlier = jnp.tril(jnp.ones((2 * B, 2 * B), jnp.int32), -1)
        matching = (chosen[:, None] == chosen[None, :]).astype(jnp.int32)
        slot_index = jnp.sum(matching * earlier, axis=1).astype(jnp.int32)
        block_index = jax.random.randint(fourth_key, (2 * B,), 0, B).astype(jnp.int32)
        return (chosen, slot_index, block_index)
    chosen, slot_index, block_index = jax.vmap(one_row)(row_keys)
    ref_table = jnp.stack([chosen[:, 0::2], slot_index[:, 0::2], chosen[:, 1::2], slot_index[:, 1::2]], axis=-1)
    ref_table = ref_table.reshape(row_count * B, 4).astype(jnp.int32)
    rows_all = jnp.arange(row_count, dtype=jnp.int32)
    section = rows_all // N_GX
    target = jnp.broadcast_to((rows_all % N_GX)[:, None], chosen.shape)
    owner_row = section[:, None] * N_GX + chosen
    send_table = jnp.full((row_count, N_GX, CAP), -1, jnp.int32)
    send_table = send_table.at[owner_row, target, slot_index].set(block_index)
    return (ref_table, send_table)


def draw_intersection_refs(key, part):
    return intersection_tables(key)[0]


def draw_send_list(key, part):
    return intersection_tables(key)[1]


def plant(entries, rng, low, top_value):
    shape = entries.shape
    place = [jax.random.randint(jax.random.fold_in(rng, axis), (), 0, shape[axis]) for axis in range(len(shape))]
    entries = entries.at[tuple(place)].set(low)
    longest = shape.index(max(shape))
    place[longest] = (place[longest] + 1) % shape[longest]
    return entries.at[tuple(place)].set(top_value)


def level_of(rng, dims, cuts, least, high):
    level = 1.0
    for axis_at, shards_of in cuts:
        steps = jax.random.uniform(jax.random.fold_in(jax.random.fold_in(rng, 6), axis_at), (shards_of,), jnp.float32, least / len(cuts), high / len(cuts))
        level = level * jnp.repeat(jnp.exp(steps), dims[axis_at] // shards_of).reshape((-1,) + (1,) * (len(dims) - 1 - axis_at))
    return level


def scatter_about(key, shape, width, most, pieces=(), kind=jnp.bfloat16):
    entries = width * jax.random.normal(key, shape, jnp.float32)
    if pieces:
        entries = entries * level_of(key, shape, pieces, -0.22, 0.18)
    return jnp.clip(entries, -most, most).astype(kind)


def setup_inputs(seed: int = 0) -> dict:
    splits = jax.random.split(jax.random.key(seed), 8)
    return {
        "les_velocity": scatter_about(splits[0], (3, NR, NA, NS), 1.0, 6.0, ((2, 4), (3, 8)), jnp.float32),
        "les_metric": jnp.clip(jnp.exp(math.log(1.5) - 1.0986123 * jax.random.uniform(splits[1], (3, NR, NA, NS), jnp.float32) ** level_of(splits[1], (3, NR, NA, NS), ((2, 4), (3, 8)), -0.2, 0.2)), 0.5, 1.5),
        "caa_state": scatter_about(splits[2], (4, NR, NA, NS), 1.0, 6.0, ((2, 4), (3, 8)), jnp.float32),
        "caa_metric": jnp.clip(jnp.exp(math.log(1.5) - 1.0986123 * jax.random.uniform(splits[3], (3, NR, NA, NS), jnp.float32) ** level_of(splits[3], (3, NR, NA, NS), ((2, 4), (3, 8)), -0.2, 0.2)), 0.5, 1.5),
        "intersection_refs": draw_intersection_refs(jax.random.fold_in(splits[7], 71), 0),
        "offsets": plant(jax.random.randint(splits[5], (SLOTS,), 0, 9), jax.random.fold_in(splits[5], 1), 0, 8).astype(jnp.int32),
        "send_list": draw_send_list(jax.random.fold_in(splits[7], 71), 0),
    }


les_step = 0.02
caa_step = 0.01
mach_number = 0.5
directions = ((3, False), (2, True), (1, False))


def slope_table():
    points = np.array([-1.0, -(0.2 ** 0.5), 0.2 ** 0.5, 1.0])
    identity = np.eye(4)
    differences = points[:, None] - points[None, :] + identity
    inverse_weights = 1.0 / np.prod(differences, axis=1)
    slope_matrix = (inverse_weights[None, :] / inverse_weights[:, None]) / differences
    slope_matrix = slope_matrix * (1.0 - identity)
    return slope_matrix - identity * slope_matrix.sum(axis=1)[:, None]


def line_slope(quantity, ghost_low, ghost_high):
    slope_matrix = jnp.asarray(slope_table(), jnp.float32)
    element_count = quantity.shape[-1] // 4
    elements = quantity.reshape(quantity.shape[:-1] + (element_count, 4))
    interior = jnp.einsum("...ej,ij->...ei", elements, slope_matrix, precision=lax.Precision.HIGHEST)
    leading = elements[..., 0]
    trailing = elements[..., 3]
    preceding = jnp.concatenate([ghost_low[..., None], trailing[..., :-1]], axis=-1)
    following = jnp.concatenate([leading[..., 1:], ghost_high[..., None]], axis=-1)
    interior = interior.at[..., 0].add(3.0 * (leading - preceding))
    interior = interior.at[..., 3].add(3.0 * (following - trailing))
    return interior.reshape(quantity.shape)


def slope(quantity, axis_dim, periodic):
    lined_up = jnp.moveaxis(quantity, axis_dim, -1)
    if periodic:
        ghost_low = lined_up[..., -1]
        ghost_high = lined_up[..., 0]
    else:
        ghost_low = jnp.zeros_like(lined_up[..., 0])
        ghost_high = jnp.zeros_like(lined_up[..., 0])
    return jnp.moveaxis(line_slope(lined_up, ghost_low, ghost_high), -1, axis_dim)


def les_rates(velocity, metric):
    slopes = []
    fluxes = []
    for direction, (axis_dim, periodic) in enumerate(directions):
        slopes.append(metric[direction][None] * slope(velocity, axis_dim, periodic))
        fluxes.append(metric[direction][None] * slope(velocity[direction][None] * velocity, axis_dim, periodic))
    change = -0.5 * sum(fluxes[j] + velocity[j][None] * slopes[j] for j in range(3))
    omega_first = slopes[1][2] - slopes[2][1]
    omega_second = slopes[2][0] - slopes[0][2]
    omega_third = slopes[0][1] - slopes[1][0]
    lamb_vector = jnp.stack([
        omega_second * velocity[2] - omega_third * velocity[1],
        omega_third * velocity[0] - omega_first * velocity[2],
        omega_first * velocity[1] - omega_second * velocity[0]])
    return change, lamb_vector


def caa_rates(acoustic, metric, source):
    stream_slope = metric[0][None] * slope(acoustic, 3, False)
    azimuth_slope = metric[1][None] * slope(jnp.stack([acoustic[0], acoustic[2]]), 2, True)
    radial_slope = metric[2][None] * slope(jnp.stack([acoustic[0], acoustic[3]]), 1, False)
    return jnp.stack([
        -(mach_number * stream_slope[0] + stream_slope[1] + azimuth_slope[1] + radial_slope[1]),
        -(mach_number * stream_slope[1] + stream_slope[0]) + source[0],
        -(mach_number * stream_slope[2] + azimuth_slope[0]) + source[1],
        -(mach_number * stream_slope[3] + radial_slope[0]) + source[2]])


def couple(lamb_vector, intersection_refs, offsets, send_list):
    rounded = lamb_vector.astype(jnp.bfloat16)
    components, radial_nodes, sector_nodes, length = rounded.shape
    block_count = length // 8
    blocks = rounded.reshape(components, radial_nodes, sector_nodes, block_count, 8).transpose(3, 0, 1, 2, 4)
    slot_rows = jnp.arange(block_count, dtype=jnp.int32) // B
    section = slot_rows // N_GX
    target = slot_rows % N_GX

    def fetch_block(owner_slab, slot_index):
        owner_row = section * N_GX + owner_slab
        return blocks[owner_row * B + send_list[owner_row, target, slot_index]].astype(jnp.float32)

    leading = fetch_block(intersection_refs[:, 0], intersection_refs[:, 1])
    trailing = fetch_block(intersection_refs[:, 2], intersection_refs[:, 3])
    fraction = offsets.astype(jnp.float32)[:, None, None, None, None]
    blended = ((8.0 - fraction) * leading + fraction * trailing) / 8.0
    return blended.transpose(1, 2, 3, 0, 4).reshape(components, radial_nodes, sector_nodes, length)


def reference(les_velocity, les_metric, caa_state, caa_metric, intersection_refs, offsets, send_list):
    velocity = les_velocity
    acoustic = caa_state
    for les_round in range(LES_STEPS):
        change, lamb_vector = les_rates(velocity, les_metric)
        source = couple(lamb_vector, intersection_refs, offsets, send_list)
        velocity = velocity + les_step * change
        for substep in range(CAA_SUB):
            acoustic = acoustic + caa_step * caa_rates(acoustic, caa_metric, source)
    return velocity, acoustic
```

```python
import functools

import jax
import jax.numpy as jnp
import numpy as np
from jax import lax
from jax.experimental import pallas as pl
from jax.experimental.pallas import tpu as pltpu
from jax.sharding import PartitionSpec as P

LES_STEPS = 2
CAA_SUB = 4

les_step = 0.02
caa_step = 0.01
mach_number = 0.5
block_nodes = 8
MESH = pl.DeviceIdType.MESH
F32 = jnp.float32
BF16 = jnp.bfloat16


def slope_table():
    points = np.array([-1.0, -(0.2**0.5), 0.2**0.5, 1.0])
    identity = np.eye(4)
    differences = points[:, None] - points[None, :] + identity
    inverse_weights = 1.0 / np.prod(differences, axis=1)
    slope_matrix = inverse_weights[None, :] / inverse_weights[:, None] / differences
    slope_matrix = slope_matrix * (1.0 - identity)
    return slope_matrix - identity * slope_matrix.sum(axis=1)[:, None]


def line_matrix(length):
    slope_matrix = slope_table()
    result = np.zeros((length + 2, length))
    for element in range(length // 4):
        at = 4 * element
        result[1 + at : 5 + at, at : at + 4] += slope_matrix.T
        result[at + 1, at] += 3.0
        result[at, at] -= 3.0
        result[at + 5, at + 3] += 3.0
        result[at + 4, at + 3] -= 3.0
    return result[1:-1].T


def halves(matrix):
    high = matrix.astype(np.float32).astype(BF16)
    low = (matrix - high.astype(np.float64)).astype(np.float32).astype(BF16)
    return high, low


def tables(radial, sector, stream):
    rows = radial * sector
    high, low = halves(line_matrix(stream).T)
    stream_mat = np.concatenate([high, high, low], axis=0)
    high, low = halves(np.kron(np.eye(radial), line_matrix(sector)))
    azimuth_mat = np.concatenate([high, high, low], axis=1)
    high, low = halves(np.kron(line_matrix(radial), np.eye(sector)))
    radial_mat = np.concatenate([high, high, low], axis=1)
    ghost = np.zeros((rows, 2 * radial))
    for r in range(radial):
        ghost[r * sector, r] = -3.0
        ghost[r * sector + sector - 1, radial + r] = 3.0
    azimuth_ghost = np.concatenate([ghost, ghost], axis=1).astype(BF16)
    ghost = np.zeros((16, 6 * stream))
    for c in range(6):
        ghost[c, c * stream] = -3.0
        ghost[8 + c, c * stream + stream - 1] = 3.0
    stream_ghost = np.concatenate([ghost, ghost], axis=0).astype(BF16)
    pick = np.zeros((16, 4 * stream))
    for c in range(4):
        pick[c, c * stream] = 1.0
        pick[8 + c, c * stream + stream - 1] = 1.0
    caa_pick = np.concatenate([pick, pick], axis=1).astype(BF16)
    pick = np.zeros((16, 3 * stream))
    for c in range(6):
        pick[c, (c % 3) * stream] = 1.0
        pick[8 + c, (c % 3) * stream + stream - 1] = 1.0
    les_pick = np.concatenate([pick, pick], axis=1).astype(BF16)
    return stream_mat, azimuth_mat, radial_mat, azimuth_ghost, stream_ghost, caa_pick, les_pick


def split(value):
    high = value.astype(BF16)
    return high, (value - high.astype(F32)).astype(BF16)


def product(left, right):
    return jnp.dot(left, right, preferred_element_type=F32)


def right_apply(fields, matrix):
    high, low = split(jnp.concatenate(fields, axis=0))
    return product(jnp.concatenate([high, low, high], axis=1), matrix)


def left_apply(matrix, fields):
    high, low = split(jnp.concatenate(fields, axis=1))
    return product(matrix, jnp.concatenate([high, low, high], axis=0))


def pick_edges(pick, fields):
    high, low = split(jnp.concatenate(fields, axis=1))
    return lax.dot_general(
        pick, jnp.concatenate([high, low], axis=1), (((1,), (1,)), ((), ())), preferred_element_type=F32
    )


def stream_fix(rim, ghost):
    high, low = split(rim)
    both = jnp.concatenate([high.astype(F32), low.astype(F32)], axis=0)
    return product(both.T.astype(BF16), ghost)


def azimuth_fix(ghost, rim):
    high, low = split(rim)
    return product(ghost, jnp.concatenate([high, low], axis=0))


def kernel(
    sizes,
    les_in, les_metric, caa_in, caa_metric, refs, offsets, send_list,
    stream_mat, azimuth_mat, radial_mat, azimuth_ghost, stream_ghost, caa_pick, les_pick,
    les_out, caa_out,
    source, weights, chooser,
    les_az_send, les_az_recv, les_st_send, les_st_recv,
    caa_az_send, caa_az_recv, caa_st_send, caa_st_recv,
    lamb_send, lamb_recv,
    les_sems, caa_sems, lamb_send_sem, lamb_recv_sem,
):
    n_sec, n_gx, n_az, radial, sector, stream, cap = sizes
    rows = radial * sector
    sec, gx, az = lax.axis_index("sec"), lax.axis_index("gx"), lax.axis_index("az")
    slabs = n_sec * n_gx
    slab = sec * n_gx + gx
    up, down = lax.rem(slab + slabs - 1, slabs), lax.rem(slab + 1, slabs)
    up_id = {"sec": up // n_gx, "gx": lax.rem(up, n_gx), "az": az}
    down_id = {"sec": down // n_gx, "gx": lax.rem(down, n_gx), "az": az}
    below_id = {"sec": sec, "gx": gx, "az": lax.rem(az + n_az - 1, n_az)}
    above_id = {"sec": sec, "gx": gx, "az": lax.rem(az + 1, n_az)}
    partners = [lax.rem(gx + k, n_gx) for k in range(1, n_gx)]

    barrier = pltpu.get_barrier_semaphore()
    for device in [up_id, down_id, below_id, above_id] + [{"sec": sec, "gx": d, "az": az} for d in partners]:
        pl.semaphore_signal(barrier, inc=1, device_id=device, device_id_type=MESH)

    lane = lax.broadcasted_iota(jnp.int32, (rows, stream), 1)
    row = lax.broadcasted_iota(jnp.int32, (rows, stream), 0)
    slot_lanes = cap * block_nodes
    groups = stream // slot_lanes
    slot_of_lane = lax.rem(lane, slot_lanes) // block_nodes
    slot_of_row = lax.rem(row, slot_lanes) // block_nodes
    node_of_lane = lax.rem(lane, block_nodes)
    same_node = lax.rem(row, block_nodes) == node_of_lane
    one_lane = lane[0:1]
    block_of_lane = one_lane // block_nodes
    lead = jnp.zeros((1, stream), jnp.int32)
    trail = jnp.zeros((1, stream), jnp.int32)
    part = jnp.zeros((1, stream), jnp.int32)
    for j in range(stream // block_nodes):
        here = block_of_lane == j
        lead = jnp.where(here, refs[j, 0] * cap + refs[j, 1], lead)
        trail = jnp.where(here, refs[j, 2] * cap + refs[j, 3], trail)
        part = jnp.where(here, offsets[j], part)
    trail_weight = part.astype(F32) / 8.0
    lead_weight = 1.0 - trail_weight
    for d in range(n_gx):
        code = slot_of_row + d * cap
        weight = jnp.where(code == lead, lead_weight, 0.0) + jnp.where(code == trail, trail_weight, 0.0)
        weights[d * stream : (d + 1) * stream, :] = jnp.where(same_node, weight, 0.0).astype(BF16)
        taken = jnp.zeros((1, stream), jnp.int32)
        for c in range(cap):
            taken = jnp.where(slot_of_lane[0:1] == c, send_list[slab, d, c], taken)
        wanted = taken * block_nodes + node_of_lane[0:1]
        chooser[:, d * stream : (d + 1) * stream] = jnp.where(row == wanted, 1.0, 0.0).astype(BF16)

    def four(sems, k, az_send, az_recv, st_send, st_recv):
        def copy(src, dst, way, device):
            return pltpu.make_async_remote_copy(
                src_ref=src.at[k, way % 2], dst_ref=dst.at[k, way % 2],
                send_sem=sems.at[k, way, 0], recv_sem=sems.at[k, way, 1],
                device_id=device, device_id_type=MESH,
            )

        return [
            copy(az_send, az_recv, 0, above_id),
            copy(az_send, az_recv, 1, below_id),
            copy(st_send, st_recv, 2, down_id),
            copy(st_send, st_recv, 3, up_id),
        ]

    def les_copies(k):
        return four(les_sems, k, les_az_send, les_az_recv, les_st_send, les_st_recv)

    def caa_copies(k):
        return four(caa_sems, k, caa_az_send, caa_az_recv, caa_st_send, caa_st_recv)

    def lamb_copy(k, d):
        return pltpu.make_async_remote_copy(
            src_ref=lamb_send.at[k, d], dst_ref=lamb_recv.at[k, gx],
            send_sem=lamb_send_sem.at[k, d], recv_sem=lamb_recv_sem.at[k, gx],
            device_id={"sec": sec, "gx": d, "az": az}, device_id_type=MESH,
        )

    def lamb_arrival(k, d):
        return pltpu.make_async_remote_copy(
            src_ref=lamb_send.at[k, d], dst_ref=lamb_recv.at[k, d],
            send_sem=lamb_send_sem.at[k, d], recv_sem=lamb_recv_sem.at[k, d],
            device_id={"sec": sec, "gx": d, "az": az}, device_id_type=MESH,
        )

    def ghosts(recv, k):
        before = jnp.where(slab > 0, recv[k, 0], 0.0)
        after = jnp.where(slab < slabs - 1, recv[k, 1], 0.0)
        return before, after

    def pieces(value, count):
        return [value[:, i * stream : (i + 1) * stream] for i in range(count)]

    pl.semaphore_wait(barrier, 4 + len(partners))

    for k in range(LES_STEPS):
        u_ref = les_in if k == 0 else les_out
        for c in range(3):
            les_az_send[k, 0, c * radial : (c + 1) * radial] = u_ref[c, pl.ds(sector - 1, radial, stride=sector), :]
            les_az_send[k, 1, c * radial : (c + 1) * radial] = u_ref[c, pl.ds(0, radial, stride=sector), :]
        copies = les_copies(k)
        copies[0].start()
        copies[1].start()
        u = [u_ref[c] for c in range(3)]
        edges = pick_edges(les_pick[...], u)
        les_st_send[k, 0] = edges[8:16]
        les_st_send[k, 1] = edges[0:8]
        copies[2].start()
        copies[3].start()

        stacked = [u + [u[j] * u[i] for i in range(3)] for j in range(3)]
        along = right_apply(stacked[0], stream_mat[...])
        along = [along[i * rows : (i + 1) * rows] for i in range(6)]
        around = pieces(left_apply(azimuth_mat[...], stacked[1]), 6)
        across = pieces(left_apply(radial_mat[...], stacked[2]), 6)

        for copy in copies:
            copy.wait_recv()
        before, after = ghosts(les_st_recv, k)
        third = lax.broadcasted_iota(jnp.int32, before.shape, 0) >= 3
        before = before * jnp.where(third, before[0:1], 1.0)
        after = after * jnp.where(third, after[0:1], 1.0)
        fix = pieces(stream_fix(jnp.concatenate([before, after], axis=0), stream_ghost[...]), 6)
        along = [a + b for a, b in zip(along, fix)]
        rim = []
        for c in range(3):
            rim.append([les_az_recv[k, way, c * radial : (c + 1) * radial] for way in range(2)])
        rim = rim + [[rim[1][way] * rim[c][way] for way in range(2)] for c in range(3)]
        rim = jnp.concatenate([jnp.concatenate(pair, axis=0) for pair in rim], axis=1)
        fix = pieces(azimuth_fix(azimuth_ghost[...], rim), 6)
        around = [a + b for a, b in zip(around, fix)]
        slopes = [
            [les_metric[0] * along[i] for i in range(3)],
            [les_metric[1] * around[i] for i in range(3)],
            [les_metric[2] * across[i] for i in range(3)],
        ]
        first = slopes[1][2] - slopes[2][1]
        second = slopes[2][0] - slopes[0][2]
        third = slopes[0][1] - slopes[1][0]
        lamb = jnp.concatenate(
            [
                second * u[2] - third * u[1],
                third * u[0] - first * u[2],
                first * u[1] - second * u[0],
            ],
            axis=0,
        ).astype(BF16)
        chosen = product(lamb, chooser[...])
        depth = 3 * rows // groups
        group_lane = lax.broadcasted_iota(jnp.int32, (depth, stream), 1) // slot_lanes
        for d in range(n_gx):
            mine = chosen[:, d * stream : (d + 1) * stream]
            packed = mine[0:depth]
            for g in range(1, groups):
                packed = jnp.where(group_lane == g, mine[g * depth : (g + 1) * depth], packed)
            lamb_send[k, d] = packed.astype(BF16)
        for d in partners:
            lamb_copy(k, d).start()
        lamb_recv[k, gx] = lamb_send[k, gx]

        for i in range(3):
            change = les_metric[0] * along[3 + i] + u[0] * slopes[0][i]
            change += les_metric[1] * around[3 + i] + u[1] * slopes[1][i]
            change += les_metric[2] * across[3 + i] + u[2] * slopes[2][i]
            les_out[i] = u[i] - (0.5 * les_step) * change

    for c in range(4):
        caa_out[c] = caa_in[c]

    def substep(k, carry):
        for way, at in ((0, sector - 1), (1, 0)):
            caa_az_send[k, way, 0:radial] = caa_out[0, pl.ds(at, radial, stride=sector), :]
            caa_az_send[k, way, radial : 2 * radial] = caa_out[2, pl.ds(at, radial, stride=sector), :]
        copies = caa_copies(k)
        copies[0].start()
        copies[1].start()
        w = [caa_out[c] for c in range(4)]
        edges = pick_edges(caa_pick[...], w)
        caa_st_send[k, 0] = edges[8:16]
        caa_st_send[k, 1] = edges[0:8]
        copies[2].start()
        copies[3].start()

        along = right_apply(w, stream_mat[...])
        along = [along[i * rows : (i + 1) * rows] for i in range(4)]
        around = pieces(left_apply(azimuth_mat[...], [w[0], w[2]]), 2)
        across = pieces(left_apply(radial_mat[...], [w[0], w[3]]), 2)

        for copy in copies:
            copy.wait_recv()
        fix = stream_fix(jnp.concatenate(ghosts(caa_st_recv, k), axis=0), stream_ghost[:, 0 : 4 * stream])
        along = [caa_metric[0] * (a + b) for a, b in zip(along, pieces(fix, 4))]
        rim = [
            jnp.concatenate([caa_az_recv[k, way, c * radial : (c + 1) * radial] for way in range(2)], axis=0)
            for c in range(2)
        ]
        fix = pieces(azimuth_fix(azimuth_ghost[...], jnp.concatenate(rim, axis=1)), 2)
        around = [caa_metric[1] * (a + b) for a, b in zip(around, fix)]
        across = [caa_metric[2] * a for a in across]
        rates = [
            mach_number * along[0] + along[1] + around[1] + across[1],
            mach_number * along[1] + along[0] - source[0:rows],
            mach_number * along[2] + around[0] - source[rows : 2 * rows],
            mach_number * along[3] + across[0] - source[2 * rows : 3 * rows],
        ]
        for c in range(4):
            caa_out[c] = w[c] - caa_step * rates[c]
        return carry

    for k in range(LES_STEPS):
        for d in partners:
            lamb_arrival(k, d).wait_recv()
        depth = 3 * rows // groups
        group_lane = lax.broadcasted_iota(jnp.int32, (depth, stream), 1) // slot_lanes
        for g in range(groups):
            got = [
                jnp.where(group_lane == g, lamb_recv[k, d].astype(F32), 0.0).astype(BF16) for d in range(n_gx)
            ]
            source[g * depth : (g + 1) * depth, :] = product(jnp.concatenate(got, axis=1), weights[...])
        lax.fori_loop(k * CAA_SUB, (k + 1) * CAA_SUB, substep, 0)

    def drain_caa(k, carry):
        for copy in caa_copies(k):
            copy.wait_send()
        return carry

    lax.fori_loop(0, LES_STEPS * CAA_SUB, drain_caa, 0)
    for k in range(LES_STEPS):
        for copy in les_copies(k):
            copy.wait_send()
        for d in partners:
            lamb_copy(k, d).wait_send()


def solution(mesh):
    n_sec, n_gx, n_az = mesh.shape["sec"], mesh.shape["gx"], mesh.shape["az"]

    def body(les_velocity, les_metric, caa_state, caa_metric, intersection_refs, offsets, send_list):
        radial, sector, stream = les_velocity.shape[1:]
        cap = send_list.shape[2]
        rows = radial * sector
        sizes = (n_sec, n_gx, n_az, radial, sector, stream, cap)
        consts = [jnp.asarray(t) for t in tables(radial, sector, stream)]
        flat = lambda x: x.reshape(x.shape[0], rows, stream)
        substeps = LES_STEPS * CAA_SUB
        depth = 3 * rows // (stream // (cap * block_nodes))
        vmem = pl.BlockSpec(memory_space=pltpu.VMEM)
        smem = pl.BlockSpec(memory_space=pltpu.SMEM)
        les_out, caa_out = pl.pallas_call(
            functools.partial(kernel, sizes),
            out_shape=(
                jax.ShapeDtypeStruct((3, rows, stream), F32),
                jax.ShapeDtypeStruct((4, rows, stream), F32),
            ),
            in_specs=[vmem] * 4 + [smem] * 3 + [vmem] * len(consts),
            out_specs=(vmem, vmem),
            scratch_shapes=[
                pltpu.VMEM((3 * rows, stream), F32),
                pltpu.VMEM((n_gx * stream, stream), BF16),
                pltpu.VMEM((rows, n_gx * stream), BF16),
                pltpu.VMEM((LES_STEPS, 2, 3 * radial, stream), F32),
                pltpu.VMEM((LES_STEPS, 2, 3 * radial, stream), F32),
                pltpu.VMEM((LES_STEPS, 2, 8, rows), F32),
                pltpu.VMEM((LES_STEPS, 2, 8, rows), F32),
                pltpu.VMEM((substeps, 2, 2 * radial, stream), F32),
                pltpu.VMEM((substeps, 2, 2 * radial, stream), F32),
                pltpu.VMEM((substeps, 2, 8, rows), F32),
                pltpu.VMEM((substeps, 2, 8, rows), F32),
                pltpu.VMEM((LES_STEPS, n_gx, depth, stream), BF16),
                pltpu.VMEM((LES_STEPS, n_gx, depth, stream), BF16),
                pltpu.SemaphoreType.DMA((LES_STEPS, 4, 2)),
                pltpu.SemaphoreType.DMA((substeps, 4, 2)),
                pltpu.SemaphoreType.DMA((LES_STEPS, n_gx)),
                pltpu.SemaphoreType.DMA((LES_STEPS, n_gx)),
            ],
            compiler_params=pltpu.CompilerParams(
                collective_id=0, has_side_effects=True, vmem_limit_bytes=40 * 2**20
            ),
        )(
            flat(les_velocity), flat(les_metric), flat(caa_state), flat(caa_metric),
            intersection_refs, offsets, send_list, *consts,
        )
        return les_out.reshape(les_velocity.shape), caa_out.reshape(caa_state.shape)

    in_specs = (
        P(None, None, "az", ("sec", "gx")),
        P(None, None, "az", ("sec", "gx")),
        P(None, None, "az", ("sec", "gx")),
        P(None, None, "az", ("sec", "gx")),
        P(("sec", "gx"), None),
        P(("sec", "gx")),
        P(),
    )
    out_specs = (P(None, None, "az", ("sec", "gx")), P(None, None, "az", ("sec", "gx")))
    return jax.shard_map(body, mesh=mesh, in_specs=in_specs, out_specs=out_specs, check_vma=False)
```

```python
import functools

import jax
import jax.numpy as jnp
import numpy as np
from jax import lax
from jax.experimental import pallas as pl
from jax.experimental.pallas import tpu as pltpu
from jax.sharding import PartitionSpec as P

LES_STEPS = 2
CAA_SUB = 4

les_step = 0.02
caa_step = 0.01
mach_number = 0.5
block_nodes = 8
MESH = pl.DeviceIdType.MESH
F32 = jnp.float32
BF16 = jnp.bfloat16


def slope_table():
    points = np.array([-1.0, -(0.2**0.5), 0.2**0.5, 1.0])
    identity = np.eye(4)
    differences = points[:, None] - points[None, :] + identity
    inverse_weights = 1.0 / np.prod(differences, axis=1)
    slope_matrix = inverse_weights[None, :] / inverse_weights[:, None] / differences
    slope_matrix = slope_matrix * (1.0 - identity)
    return slope_matrix - identity * slope_matrix.sum(axis=1)[:, None]


def line_matrix(length):
    slope_matrix = slope_table()
    result = np.zeros((length + 2, length))
    for element in range(length // 4):
        at = 4 * element
        result[1 + at : 5 + at, at : at + 4] += slope_matrix.T
        result[at + 1, at] += 3.0
        result[at, at] -= 3.0
        result[at + 5, at + 3] += 3.0
        result[at + 4, at + 3] -= 3.0
    return result[1:-1].T


def halves(matrix):
    high = matrix.astype(np.float32).astype(BF16)
    low = (matrix - high.astype(np.float64)).astype(np.float32).astype(BF16)
    return high, low


def tables(radial, sector, stream):
    rows = radial * sector
    high, low = halves(line_matrix(stream).T)
    stream_mat = np.concatenate([high, high, low], axis=0)
    high, low = halves(np.kron(np.eye(radial), line_matrix(sector)))
    azimuth_mat = np.concatenate([high, high, low], axis=1)
    high, low = halves(np.kron(line_matrix(radial), np.eye(sector)))
    radial_mat = np.concatenate([high, high, low], axis=1)
    ghost = np.zeros((rows, 2 * radial))
    for r in range(radial):
        ghost[r * sector, r] = -3.0
        ghost[r * sector + sector - 1, radial + r] = 3.0
    azimuth_ghost = np.concatenate([ghost, ghost], axis=1).astype(BF16)
    ghost = np.zeros((16, 6 * stream))
    for c in range(6):
        ghost[c, c * stream] = -3.0
        ghost[8 + c, c * stream + stream - 1] = 3.0
    stream_ghost = np.concatenate([ghost, ghost], axis=0).astype(BF16)
    pick = np.zeros((16, 4 * stream))
    for c in range(4):
        pick[c, c * stream] = 1.0
        pick[8 + c, c * stream + stream - 1] = 1.0
    caa_pick = np.concatenate([pick, pick], axis=1).astype(BF16)
    pick = np.zeros((16, 3 * stream))
    for c in range(6):
        pick[c, (c % 3) * stream] = 1.0
        pick[8 + c, (c % 3) * stream + stream - 1] = 1.0
    les_pick = np.concatenate([pick, pick], axis=1).astype(BF16)
    wide = [azimuth_mat, radial_mat, stream_ghost, caa_pick, les_pick]
    azimuth_mat, radial_mat, stream_ghost, caa_pick, les_pick = [tall(t, stream) for t in wide]
    return stream_mat, azimuth_mat, radial_mat, azimuth_ghost, stream_ghost, caa_pick, les_pick


def tall(table, width):
    return np.concatenate([table[:, i : i + width] for i in range(0, table.shape[1], width)], axis=0)


def wide(ref, height, count=None):
    count = ref.shape[0] // height if count is None else count
    return jnp.concatenate([ref[i * height : (i + 1) * height, :] for i in range(count)], axis=1)


def split(value):
    high = value.astype(BF16)
    return high, (value - high.astype(F32)).astype(BF16)


def product(left, right):
    return jnp.dot(left, right, preferred_element_type=F32)


def right_apply(fields, matrix):
    high, low = split(jnp.concatenate(fields, axis=0))
    return product(jnp.concatenate([high, low, high], axis=1), matrix)


def left_apply(matrix, fields):
    high, low = split(jnp.concatenate(fields, axis=1))
    return product(matrix, jnp.concatenate([high, low, high], axis=0))


def pick_edges(pick, fields):
    high, low = split(jnp.concatenate(fields, axis=1))
    return lax.dot_general(
        pick, jnp.concatenate([high, low], axis=1), (((1,), (1,)), ((), ())), preferred_element_type=F32
    )


def stream_fix(rim, ghost):
    high, low = split(rim)
    both = jnp.concatenate([high.astype(F32), low.astype(F32)], axis=0)
    return product(both.T.astype(BF16), ghost)


def azimuth_fix(ghost, rim):
    high, low = split(rim)
    return product(ghost, jnp.concatenate([high, low], axis=0))


def kernel(
    sizes,
    les_hbm, les_metric_hbm, caa_hbm, caa_metric_hbm, refs_hbm, offsets_hbm, send_list_hbm,
    stream_mat_hbm, azimuth_mat_hbm, radial_mat_hbm, azimuth_ghost_hbm, stream_ghost_hbm, caa_pick_hbm, les_pick_hbm,
    les_out, caa_out,
    les_in, les_metric, caa_metric, refs, offsets, send_list,
    stream_mat, azimuth_mat, radial_mat, azimuth_ghost, stream_ghost, caa_pick, les_pick,
    load_sems,
    source, weights, chooser,
    les_az_send, les_az_recv, les_st_send, les_st_recv,
    caa_az_send, caa_az_recv, caa_st_send, caa_st_recv,
    lamb_send, lamb_recv,
    les_sems, caa_sems, lamb_send_sem, lamb_recv_sem,
):
    n_sec, n_gx, n_az, radial, sector, stream, cap = sizes
    rows = radial * sector
    sec, gx, az = lax.axis_index("sec"), lax.axis_index("gx"), lax.axis_index("az")
    slabs = n_sec * n_gx
    slab = sec * n_gx + gx
    up, down = lax.rem(slab + slabs - 1, slabs), lax.rem(slab + 1, slabs)
    up_id = {"sec": up // n_gx, "gx": lax.rem(up, n_gx), "az": az}
    down_id = {"sec": down // n_gx, "gx": lax.rem(down, n_gx), "az": az}
    below_id = {"sec": sec, "gx": gx, "az": lax.rem(az + n_az - 1, n_az)}
    above_id = {"sec": sec, "gx": gx, "az": lax.rem(az + 1, n_az)}
    partners = [lax.rem(gx + k, n_gx) for k in range(1, n_gx)]

    barrier = pltpu.get_barrier_semaphore()
    for device in [up_id, down_id, below_id, above_id] + [{"sec": sec, "gx": d, "az": az} for d in partners]:
        pl.semaphore_signal(barrier, inc=1, device_id=device, device_id_type=MESH)

    loads = [
        pltpu.make_async_copy(src, dst, load_sems.at[i])
        for i, (src, dst) in enumerate(
            [
                (refs_hbm, refs), (offsets_hbm, offsets), (send_list_hbm, send_list),
                (les_hbm, les_in), (les_pick_hbm, les_pick),
                (stream_mat_hbm, stream_mat), (azimuth_mat_hbm, azimuth_mat), (radial_mat_hbm, radial_mat),
                (azimuth_ghost_hbm, azimuth_ghost), (stream_ghost_hbm, stream_ghost),
                (les_metric_hbm, les_metric), (caa_hbm, caa_out), (caa_pick_hbm, caa_pick),
                (caa_metric_hbm, caa_metric),
            ]
        )
    ]
    for load in loads:
        load.start()
    for load in loads[0:3]:
        load.wait()

    lane = lax.broadcasted_iota(jnp.int32, (rows, stream), 1)
    row = lax.broadcasted_iota(jnp.int32, (rows, stream), 0)
    slot_lanes = cap * block_nodes
    groups = stream // slot_lanes
    slot_of_lane = lax.rem(lane, slot_lanes) // block_nodes
    slot_of_row = lax.rem(row, slot_lanes) // block_nodes
    node_of_lane = lax.rem(lane, block_nodes)
    same_node = lax.rem(row, block_nodes) == node_of_lane
    one_lane = lane[0:1]
    block_of_lane = one_lane // block_nodes
    lead = jnp.zeros((1, stream), jnp.int32)
    trail = jnp.zeros((1, stream), jnp.int32)
    part = jnp.zeros((1, stream), jnp.int32)
    for j in range(stream // block_nodes):
        here = block_of_lane == j
        lead = jnp.where(here, refs[0, j] * cap + refs[1, j], lead)
        trail = jnp.where(here, refs[2, j] * cap + refs[3, j], trail)
        part = jnp.where(here, offsets[j], part)
    trail_weight = part.astype(F32) / 8.0
    lead_weight = 1.0 - trail_weight
    for d in range(n_gx):
        code = slot_of_row + d * cap
        weight = jnp.where(code == lead, lead_weight, 0.0) + jnp.where(code == trail, trail_weight, 0.0)
        weights[d * stream : (d + 1) * stream, :] = jnp.where(same_node, weight, 0.0).astype(BF16)
        taken = jnp.zeros((1, stream), jnp.int32)
        for c in range(cap):
            taken = jnp.where(slot_of_lane[0:1] == c, send_list[slab, d, c], taken)
        wanted = taken * block_nodes + node_of_lane[0:1]
        chooser[:, d * stream : (d + 1) * stream] = jnp.where(row == wanted, 1.0, 0.0).astype(BF16)

    def four(sems, k, az_send, az_recv, st_send, st_recv):
        def copy(src, dst, way, device):
            return pltpu.make_async_remote_copy(
                src_ref=src.at[k, way % 2], dst_ref=dst.at[k, way % 2],
                send_sem=sems.at[k, way, 0], recv_sem=sems.at[k, way, 1],
                device_id=device, device_id_type=MESH,
            )

        return [
            copy(az_send, az_recv, 0, above_id),
            copy(az_send, az_recv, 1, below_id),
            copy(st_send, st_recv, 2, down_id),
            copy(st_send, st_recv, 3, up_id),
        ]

    def les_copies(k):
        return four(les_sems, k, les_az_send, les_az_recv, les_st_send, les_st_recv)

    def caa_copies(k):
        return four(caa_sems, k, caa_az_send, caa_az_recv, caa_st_send, caa_st_recv)

    def lamb_copy(k, d):
        return pltpu.make_async_remote_copy(
            src_ref=lamb_send.at[k, d], dst_ref=lamb_recv.at[k, gx],
            send_sem=lamb_send_sem.at[k, d], recv_sem=lamb_recv_sem.at[k, gx],
            device_id={"sec": sec, "gx": d, "az": az}, device_id_type=MESH,
        )

    def lamb_arrival(k, d):
        return pltpu.make_async_remote_copy(
            src_ref=lamb_send.at[k, d], dst_ref=lamb_recv.at[k, d],
            send_sem=lamb_send_sem.at[k, d], recv_sem=lamb_recv_sem.at[k, d],
            device_id={"sec": sec, "gx": d, "az": az}, device_id_type=MESH,
        )

    def ghosts(recv, k):
        before = jnp.where(slab > 0, recv[k, 0], 0.0)
        after = jnp.where(slab < slabs - 1, recv[k, 1], 0.0)
        return before, after

    def pieces(value, count):
        return [value[:, i * stream : (i + 1) * stream] for i in range(count)]

    for load in loads[3:]:
        load.wait()
    pl.semaphore_wait(barrier, 4 + len(partners))

    for k in range(LES_STEPS):
        u_ref = les_in if k == 0 else les_out
        for c in range(3):
            les_az_send[k, 0, c * radial : (c + 1) * radial] = u_ref[c, pl.ds(sector - 1, radial, stride=sector), :]
            les_az_send[k, 1, c * radial : (c + 1) * radial] = u_ref[c, pl.ds(0, radial, stride=sector), :]
        copies = les_copies(k)
        copies[0].start()
        copies[1].start()
        u = [u_ref[c] for c in range(3)]
        edges = pick_edges(wide(les_pick, 16), u)
        les_st_send[k, 0] = edges[8:16]
        les_st_send[k, 1] = edges[0:8]
        copies[2].start()
        copies[3].start()

        stacked = [u + [u[j] * u[i] for i in range(3)] for j in range(3)]
        along = right_apply(stacked[0], stream_mat[...])
        along = [along[i * rows : (i + 1) * rows] for i in range(6)]
        around = pieces(left_apply(wide(azimuth_mat, rows), stacked[1]), 6)
        across = pieces(left_apply(wide(radial_mat, rows), stacked[2]), 6)

        for copy in copies:
            copy.wait_recv()
        before, after = ghosts(les_st_recv, k)
        third = lax.broadcasted_iota(jnp.int32, before.shape, 0) >= 3
        before = before * jnp.where(third, before[0:1], 1.0)
        after = after * jnp.where(third, after[0:1], 1.0)
        fix = pieces(stream_fix(jnp.concatenate([before, after], axis=0), wide(stream_ghost, 32)), 6)
        along = [a + b for a, b in zip(along, fix)]
        rim = []
        for c in range(3):
            rim.append([les_az_recv[k, way, c * radial : (c + 1) * radial] for way in range(2)])
        rim = rim + [[rim[1][way] * rim[c][way] for way in range(2)] for c in range(3)]
        rim = jnp.concatenate([jnp.concatenate(pair, axis=0) for pair in rim], axis=1)
        fix = pieces(azimuth_fix(azimuth_ghost[...], rim), 6)
        around = [a + b for a, b in zip(around, fix)]
        slopes = [
            [les_metric[0] * along[i] for i in range(3)],
            [les_metric[1] * around[i] for i in range(3)],
            [les_metric[2] * across[i] for i in range(3)],
        ]
        first = slopes[1][2] - slopes[2][1]
        second = slopes[2][0] - slopes[0][2]
        third = slopes[0][1] - slopes[1][0]
        lamb = jnp.concatenate(
            [
                second * u[2] - third * u[1],
                third * u[0] - first * u[2],
                first * u[1] - second * u[0],
            ],
            axis=0,
        ).astype(BF16)
        chosen = product(lamb, chooser[...])
        depth = 3 * rows // groups
        group_lane = lax.broadcasted_iota(jnp.int32, (depth, stream), 1) // slot_lanes
        for d in range(n_gx):
            mine = chosen[:, d * stream : (d + 1) * stream]
            packed = mine[0:depth]
            for g in range(1, groups):
                packed = jnp.where(group_lane == g, mine[g * depth : (g + 1) * depth], packed)
            lamb_send[k, d] = packed.astype(BF16)
        for d in partners:
            lamb_copy(k, d).start()
        lamb_recv[k, gx] = lamb_send[k, gx]

        for i in range(3):
            change = les_metric[0] * along[3 + i] + u[0] * slopes[0][i]
            change += les_metric[1] * around[3 + i] + u[1] * slopes[1][i]
            change += les_metric[2] * across[3 + i] + u[2] * slopes[2][i]
            les_out[i] = u[i] - (0.5 * les_step) * change

    def substep(k, carry):
        for way, at in ((0, sector - 1), (1, 0)):
            caa_az_send[k, way, 0:radial] = caa_out[0, pl.ds(at, radial, stride=sector), :]
            caa_az_send[k, way, radial : 2 * radial] = caa_out[2, pl.ds(at, radial, stride=sector), :]
        copies = caa_copies(k)
        copies[0].start()
        copies[1].start()
        w = [caa_out[c] for c in range(4)]
        edges = pick_edges(wide(caa_pick, 16), w)
        caa_st_send[k, 0] = edges[8:16]
        caa_st_send[k, 1] = edges[0:8]
        copies[2].start()
        copies[3].start()

        along = right_apply(w, stream_mat[...])
        along = [along[i * rows : (i + 1) * rows] for i in range(4)]
        around = pieces(left_apply(wide(azimuth_mat, rows), [w[0], w[2]]), 2)
        across = pieces(left_apply(wide(radial_mat, rows), [w[0], w[3]]), 2)

        for copy in copies:
            copy.wait_recv()
        fix = stream_fix(jnp.concatenate(ghosts(caa_st_recv, k), axis=0), wide(stream_ghost, 32, 4))
        along = [caa_metric[0] * (a + b) for a, b in zip(along, pieces(fix, 4))]
        rim = [
            jnp.concatenate([caa_az_recv[k, way, c * radial : (c + 1) * radial] for way in range(2)], axis=0)
            for c in range(2)
        ]
        fix = pieces(azimuth_fix(azimuth_ghost[...], jnp.concatenate(rim, axis=1)), 2)
        around = [caa_metric[1] * (a + b) for a, b in zip(around, fix)]
        across = [caa_metric[2] * a for a in across]
        rates = [
            mach_number * along[0] + along[1] + around[1] + across[1],
            mach_number * along[1] + along[0] - source[0:rows],
            mach_number * along[2] + around[0] - source[rows : 2 * rows],
            mach_number * along[3] + across[0] - source[2 * rows : 3 * rows],
        ]
        for c in range(4):
            caa_out[c] = w[c] - caa_step * rates[c]
        return carry

    for k in range(LES_STEPS):
        for d in partners:
            lamb_arrival(k, d).wait_recv()
        depth = 3 * rows // groups
        group_lane = lax.broadcasted_iota(jnp.int32, (depth, stream), 1) // slot_lanes
        for g in range(groups):
            got = [
                jnp.where(group_lane == g, lamb_recv[k, d].astype(F32), 0.0).astype(BF16) for d in range(n_gx)
            ]
            source[g * depth : (g + 1) * depth, :] = product(jnp.concatenate(got, axis=1), weights[...])
        lax.fori_loop(k * CAA_SUB, (k + 1) * CAA_SUB, substep, 0)

    def drain_caa(k, carry):
        for copy in caa_copies(k):
            copy.wait_send()
        return carry

    lax.fori_loop(0, LES_STEPS * CAA_SUB, drain_caa, 0)
    for k in range(LES_STEPS):
        for copy in les_copies(k):
            copy.wait_send()
        for d in partners:
            lamb_copy(k, d).wait_send()


def hand_over(les_from, caa_from, les_to, caa_to, sems):
    copies = [
        pltpu.make_async_copy(les_from, les_to, sems.at[0]),
        pltpu.make_async_copy(caa_from, caa_to, sems.at[1]),
    ]
    for copy in copies:
        copy.start()
    for copy in copies:
        copy.wait()


def solution(mesh):
    n_sec, n_gx, n_az = mesh.shape["sec"], mesh.shape["gx"], mesh.shape["az"]

    def body(les_velocity, les_metric, caa_state, caa_metric, intersection_refs, offsets, send_list):
        radial, sector, stream = les_velocity.shape[1:]
        cap = send_list.shape[2]
        rows = radial * sector
        sizes = (n_sec, n_gx, n_az, radial, sector, stream, cap)
        consts = [jnp.asarray(t) for t in tables(radial, sector, stream)]
        flat = lambda x: x.reshape(x.shape[0], rows, stream)
        substeps = LES_STEPS * CAA_SUB
        depth = 3 * rows // (stream // (cap * block_nodes))
        vmem = pl.BlockSpec(memory_space=pltpu.VMEM)
        hbm = pl.BlockSpec(memory_space=pltpu.HBM)
        les_out, caa_out = pl.pallas_call(
            functools.partial(kernel, sizes),
            out_shape=(
                jax.ShapeDtypeStruct((3, rows, stream), F32),
                jax.ShapeDtypeStruct((4, rows, stream), F32),
            ),
            in_specs=[hbm] * (7 + len(consts)),
            out_specs=(vmem, vmem),
            scratch_shapes=[
                pltpu.VMEM((3, rows, stream), F32),
                pltpu.VMEM((3, rows, stream), F32),
                pltpu.VMEM((3, rows, stream), F32),
                pltpu.SMEM(intersection_refs.shape[::-1], jnp.int32),
                pltpu.SMEM(offsets.shape, jnp.int32),
                pltpu.SMEM(send_list.shape, jnp.int32),
            ]
            + [pltpu.VMEM(t.shape, BF16) for t in consts]
            + [
                pltpu.SemaphoreType.DMA((7 + len(consts),)),
                pltpu.VMEM((3 * rows, stream), F32),
                pltpu.VMEM((n_gx * stream, stream), BF16),
                pltpu.VMEM((rows, n_gx * stream), BF16),
                pltpu.VMEM((LES_STEPS, 2, 3 * radial, stream), F32),
                pltpu.VMEM((LES_STEPS, 2, 3 * radial, stream), F32),
                pltpu.VMEM((LES_STEPS, 2, 8, rows), F32),
                pltpu.VMEM((LES_STEPS, 2, 8, rows), F32),
                pltpu.VMEM((substeps, 2, 2 * radial, stream), F32),
                pltpu.VMEM((substeps, 2, 2 * radial, stream), F32),
                pltpu.VMEM((substeps, 2, 8, rows), F32),
                pltpu.VMEM((substeps, 2, 8, rows), F32),
                pltpu.VMEM((LES_STEPS, n_gx, depth, stream), BF16),
                pltpu.VMEM((LES_STEPS, n_gx, depth, stream), BF16),
                pltpu.SemaphoreType.DMA((LES_STEPS, 4, 2)),
                pltpu.SemaphoreType.DMA((substeps, 4, 2)),
                pltpu.SemaphoreType.DMA((LES_STEPS, n_gx)),
                pltpu.SemaphoreType.DMA((LES_STEPS, n_gx)),
            ],
            compiler_params=pltpu.CompilerParams(
                collective_id=0, has_side_effects=True, vmem_limit_bytes=63 * 2**20
            ),
        )(
            flat(les_velocity), flat(les_metric), flat(caa_state), flat(caa_metric),
            intersection_refs.T, offsets, send_list, *consts,
        )
        les_out, caa_out = pl.pallas_call(
            hand_over,
            out_shape=(
                jax.ShapeDtypeStruct((3, rows, stream), F32),
                jax.ShapeDtypeStruct((4, rows, stream), F32),
            ),
            in_specs=[hbm] * 2,
            out_specs=(hbm, hbm),
            scratch_shapes=[pltpu.SemaphoreType.DMA((2,))],
            compiler_params=pltpu.CompilerParams(vmem_limit_bytes=63 * 2**20),
        )(les_out, caa_out)
        return les_out.reshape(les_velocity.shape), caa_out.reshape(caa_state.shape)

    in_specs = (
        P(None, None, "az", ("sec", "gx")),
        P(None, None, "az", ("sec", "gx")),
        P(None, None, "az", ("sec", "gx")),
        P(None, None, "az", ("sec", "gx")),
        P(("sec", "gx"), None),
        P(("sec", "gx")),
        P(),
    )
    out_specs = (P(None, None, "az", ("sec", "gx")), P(None, None, "az", ("sec", "gx")))
    return jax.shard_map(body, mesh=mesh, in_specs=in_specs, out_specs=out_specs, check_vma=False)
```

```python
import functools

import jax
import jax.numpy as jnp
import numpy as np
from jax import lax
from jax.experimental import pallas as pl
from jax.experimental.pallas import tpu as pltpu
from jax.sharding import PartitionSpec as P

LES_STEPS = 2
CAA_SUB = 4

les_step = 0.02
caa_step = 0.01
mach_number = 0.5
block_nodes = 8
margin_nodes = 16
MESH = pl.DeviceIdType.MESH
F32 = jnp.float32
BF16 = jnp.bfloat16


def slope_table():
    points = np.array([-1.0, -(0.2**0.5), 0.2**0.5, 1.0])
    identity = np.eye(4)
    differences = points[:, None] - points[None, :] + identity
    inverse_weights = 1.0 / np.prod(differences, axis=1)
    slope_matrix = inverse_weights[None, :] / inverse_weights[:, None] / differences
    slope_matrix = slope_matrix * (1.0 - identity)
    return slope_matrix - identity * slope_matrix.sum(axis=1)[:, None]


def line_matrix(length):
    slope_matrix = slope_table()
    result = np.zeros((length + 2, length))
    for element in range(length // 4):
        at = 4 * element
        result[1 + at : 5 + at, at : at + 4] += slope_matrix.T
        result[at + 1, at] += 3.0
        result[at, at] -= 3.0
        result[at + 5, at + 3] += 3.0
        result[at + 4, at + 3] -= 3.0
    return result[1:-1].T


def halves(matrix):
    high = matrix.astype(np.float32).astype(BF16)
    low = (matrix - high.astype(np.float64)).astype(np.float32).astype(BF16)
    return high, low


def tables(radial, sector, stream):
    rows = radial * sector
    high, low = halves(line_matrix(stream).T)
    stream_mat = np.concatenate([high, high, low], axis=0)
    high, low = halves(np.kron(np.eye(radial), line_matrix(sector)))
    azimuth_mat = np.concatenate([high, high, low], axis=1)
    high, low = halves(np.kron(line_matrix(radial), np.eye(sector)))
    radial_mat = np.concatenate([high, high, low], axis=1)
    ghost = np.zeros((rows, 2 * radial))
    for r in range(radial):
        ghost[r * sector, r] = -3.0
        ghost[r * sector + sector - 1, radial + r] = 3.0
    azimuth_ghost = np.concatenate([ghost, ghost], axis=1).astype(BF16)
    ghost = np.zeros((16, 6 * stream))
    for c in range(6):
        ghost[c, c * stream] = -3.0
        ghost[8 + c, c * stream + stream - 1] = 3.0
    stream_ghost = np.concatenate([ghost, ghost], axis=0).astype(BF16)
    pick = np.zeros((16, 3 * stream))
    for c in range(6):
        pick[c, (c % 3) * stream] = 1.0
        pick[8 + c, (c % 3) * stream + stream - 1] = 1.0
    les_pick = np.concatenate([pick, pick], axis=1).astype(BF16)
    m = margin_nodes
    inner = np.zeros((stream, 4 * stream))
    mix = mach_number * np.eye(4)
    mix[1, 0] = mix[0, 1] = 1.0
    joint = np.zeros((4, stream, stream))
    spread = np.zeros((stream, 3 * stream))
    for c in range(4):
        inner[2 * m * c + m - 1, c * stream] = -3.0
        inner[2 * m * c + m, c * stream + stream - 1] = 3.0
        for o in range(4):
            joint[c, 0, 2 * m * o + m - 1] = 3.0 * mix[c, o]
            joint[c, stream - 1, 2 * m * o + m] = -3.0 * mix[c, o]
            if c < 3:
                for t in range(2 * m):
                    spread[2 * m * c + t, c * stream + 2 * m * o + t] = 1.0
    high, low = halves(np.kron(mix, np.kron(np.eye(2), line_matrix(m).T)))
    joint = [joint[c // 2].astype(BF16) for c in range(8)]
    margin_mat = np.concatenate([high, high, low] + joint, axis=0)
    columns = [azimuth_mat, radial_mat, stream_ghost, les_pick, inner.astype(BF16), spread.astype(BF16)]
    return [stream_mat, azimuth_ghost, margin_mat] + [tall(t, stream) for t in columns]


def tall(table, width):
    return np.concatenate([table[:, i : i + width] for i in range(0, table.shape[1], width)], axis=0)


def wide(ref, height, count=None):
    count = ref.shape[0] // height if count is None else count
    return jnp.concatenate([ref[i * height : (i + 1) * height, :] for i in range(count)], axis=1)


def split(value):
    high = value.astype(BF16)
    return high, (value - high.astype(F32)).astype(BF16)


def product(left, right):
    return jnp.dot(left, right, preferred_element_type=F32)


def right_apply(fields, matrix):
    high, low = split(jnp.concatenate(fields, axis=0))
    return product(jnp.concatenate([high, low, high], axis=1), matrix)


def left_apply(matrix, fields):
    high, low = split(jnp.concatenate(fields, axis=1))
    return product(matrix, jnp.concatenate([high, low, high], axis=0))


def pick_edges(pick, fields):
    high, low = split(jnp.concatenate(fields, axis=1))
    return lax.dot_general(
        pick, jnp.concatenate([high, low], axis=1), (((1,), (1,)), ((), ())), preferred_element_type=F32
    )


def stream_fix(rim, ghost):
    high, low = split(rim)
    both = jnp.concatenate([high.astype(F32), low.astype(F32)], axis=0)
    return product(both.T.astype(BF16), ghost)


def azimuth_fix(ghost, rim):
    high, low = split(rim)
    return product(ghost, jnp.concatenate([high, low], axis=0))


def kernel(
    sizes,
    les_hbm, les_metric_hbm, caa_hbm, caa_metric_hbm, refs_hbm, offsets_hbm, send_list_hbm,
    stream_mat_hbm, azimuth_ghost_hbm, margin_mat_hbm,
    azimuth_mat_hbm, radial_mat_hbm, stream_ghost_hbm, les_pick_hbm, inner_hbm, spread_hbm,
    les_out, caa_out,
    les_in, les_metric, caa_metric, refs, offsets, send_list,
    stream_mat, azimuth_ghost, margin_mat, azimuth_mat, radial_mat, stream_ghost, les_pick, inner, spread,
    load_sems,
    source, weights, chooser,
    les_az_send, les_az_recv, les_st_send, les_st_recv,
    caa_az_send, caa_az_recv, margin_send, margin_recv, margin, margin_metric, margin_source,
    lamb_send, lamb_recv,
    les_sems, caa_sems, margin_sems, lamb_send_sem, lamb_recv_sem,
):
    n_sec, n_gx, n_az, radial, sector, stream, cap = sizes
    rows = radial * sector
    sec, gx, az = lax.axis_index("sec"), lax.axis_index("gx"), lax.axis_index("az")
    slabs = n_sec * n_gx
    slab = sec * n_gx + gx
    up, down = lax.rem(slab + slabs - 1, slabs), lax.rem(slab + 1, slabs)
    up_id = {"sec": up // n_gx, "gx": lax.rem(up, n_gx), "az": az}
    down_id = {"sec": down // n_gx, "gx": lax.rem(down, n_gx), "az": az}
    below_id = {"sec": sec, "gx": gx, "az": lax.rem(az + n_az - 1, n_az)}
    above_id = {"sec": sec, "gx": gx, "az": lax.rem(az + 1, n_az)}
    partners = [lax.rem(gx + k, n_gx) for k in range(1, n_gx)]

    barrier = pltpu.get_barrier_semaphore()
    for device in [up_id, down_id, below_id, above_id] + [{"sec": sec, "gx": d, "az": az} for d in partners]:
        pl.semaphore_signal(barrier, inc=1, device_id=device, device_id_type=MESH)

    loads = [
        pltpu.make_async_copy(src, dst, load_sems.at[i])
        for i, (src, dst) in enumerate(
            [
                (refs_hbm, refs), (offsets_hbm, offsets), (send_list_hbm, send_list),
                (les_hbm, les_in), (les_pick_hbm, les_pick),
                (stream_mat_hbm, stream_mat), (azimuth_mat_hbm, azimuth_mat), (radial_mat_hbm, radial_mat),
                (azimuth_ghost_hbm, azimuth_ghost), (stream_ghost_hbm, stream_ghost),
                (les_metric_hbm, les_metric), (caa_hbm, caa_out), (margin_mat_hbm, margin_mat), (inner_hbm, inner), (spread_hbm, spread),
                (caa_metric_hbm, caa_metric),
            ]
        )
    ]
    for load in loads:
        load.start()
    for load in loads[0:3]:
        load.wait()

    lane = lax.broadcasted_iota(jnp.int32, (rows, stream), 1)
    row = lax.broadcasted_iota(jnp.int32, (rows, stream), 0)
    slot_lanes = cap * block_nodes
    groups = stream // slot_lanes
    slot_of_lane = lax.rem(lane, slot_lanes) // block_nodes
    slot_of_row = lax.rem(row, slot_lanes) // block_nodes
    node_of_lane = lax.rem(lane, block_nodes)
    same_node = lax.rem(row, block_nodes) == node_of_lane
    one_lane = lane[0:1]
    block_of_lane = one_lane // block_nodes
    lead = jnp.zeros((1, stream), jnp.int32)
    trail = jnp.zeros((1, stream), jnp.int32)
    part = jnp.zeros((1, stream), jnp.int32)
    for j in range(stream // block_nodes):
        here = block_of_lane == j
        lead = jnp.where(here, refs[0, j] * cap + refs[1, j], lead)
        trail = jnp.where(here, refs[2, j] * cap + refs[3, j], trail)
        part = jnp.where(here, offsets[j], part)
    trail_weight = part.astype(F32) / 8.0
    lead_weight = 1.0 - trail_weight
    for d in range(n_gx):
        code = slot_of_row + d * cap
        weight = jnp.where(code == lead, lead_weight, 0.0) + jnp.where(code == trail, trail_weight, 0.0)
        weights[d * stream : (d + 1) * stream, :] = jnp.where(same_node, weight, 0.0).astype(BF16)
        taken = jnp.zeros((1, stream), jnp.int32)
        for c in range(cap):
            taken = jnp.where(slot_of_lane[0:1] == c, send_list[slab, d, c], taken)
        wanted = taken * block_nodes + node_of_lane[0:1]
        chooser[:, d * stream : (d + 1) * stream] = jnp.where(row == wanted, 1.0, 0.0).astype(BF16)

    def pair(sems, k, first, send, recv, devices):
        return [
            pltpu.make_async_remote_copy(
                src_ref=send.at[k, way], dst_ref=recv.at[k, way],
                send_sem=sems.at[k, first + way, 0], recv_sem=sems.at[k, first + way, 1],
                device_id=devices[way], device_id_type=MESH,
            )
            for way in range(2)
        ]

    def les_copies(k):
        copies = pair(les_sems, k, 0, les_az_send, les_az_recv, (above_id, below_id))
        return copies + pair(les_sems, k, 2, les_st_send, les_st_recv, (down_id, up_id))

    def caa_copies(k):
        return pair(caa_sems, k, 0, caa_az_send, caa_az_recv, (above_id, below_id))

    def margin_copies(i):
        return [
            pltpu.make_async_remote_copy(
                src_ref=margin_send.at[i], dst_ref=margin_recv.at[i, way],
                send_sem=margin_sems.at[i, way, 0], recv_sem=margin_sems.at[i, way, 1],
                device_id=(down_id, up_id)[way], device_id_type=MESH,
            )
            for way in range(2)
        ]

    width = 2 * margin_nodes
    group = lane // width

    def send_margin(i, fields, first):
        packed = jnp.zeros((rows, stream), F32)
        for c, field in enumerate(fields, first):
            packed = jnp.where(group == c, pltpu.roll(field, width * c + margin_nodes, 1), packed)
        margin_send[i] = packed.astype(BF16)
        for copy in margin_copies(i):
            copy.start()

    def take_margin(i):
        for copy in margin_copies(i):
            copy.wait_recv()
        before = jnp.where(slab > 0, margin_recv[i, 0].astype(F32), 0.0)
        after = jnp.where(slab < slabs - 1, margin_recv[i, 1].astype(F32), 0.0)
        return jnp.where(lax.rem(lane, width) < margin_nodes, before, after)

    def swap_azimuth(value):
        at = lax.broadcasted_iota(jnp.int32, value.shape, 1) // width
        return jnp.where(lax.rem(at, 2) == 0, pltpu.roll(value, 2 * width, 1), 0.0)

    def swap_radial(value):
        return jnp.where(
            group == 0, pltpu.roll(value, width, 1), jnp.where(group == 3, pltpu.roll(value, 3 * width, 1), 0.0)
        )

    def lamb_copy(k, d):
        return pltpu.make_async_remote_copy(
            src_ref=lamb_send.at[k, d], dst_ref=lamb_recv.at[k, gx],
            send_sem=lamb_send_sem.at[k, d], recv_sem=lamb_recv_sem.at[k, gx],
            device_id={"sec": sec, "gx": d, "az": az}, device_id_type=MESH,
        )

    def lamb_arrival(k, d):
        return pltpu.make_async_remote_copy(
            src_ref=lamb_send.at[k, d], dst_ref=lamb_recv.at[k, d],
            send_sem=lamb_send_sem.at[k, d], recv_sem=lamb_recv_sem.at[k, d],
            device_id={"sec": sec, "gx": d, "az": az}, device_id_type=MESH,
        )

    def ghosts(recv, k):
        before = jnp.where(slab > 0, recv[k, 0], 0.0)
        after = jnp.where(slab < slabs - 1, recv[k, 1], 0.0)
        return before, after

    def pieces(value, count):
        return [value[:, i * stream : (i + 1) * stream] for i in range(count)]

    for load in loads[3:]:
        load.wait()
    pl.semaphore_wait(barrier, 4 + len(partners))

    for k in range(LES_STEPS):
        u_ref = les_in if k == 0 else les_out
        for c in range(3):
            les_az_send[k, 0, c * radial : (c + 1) * radial] = u_ref[c, pl.ds(sector - 1, radial, stride=sector), :]
            les_az_send[k, 1, c * radial : (c + 1) * radial] = u_ref[c, pl.ds(0, radial, stride=sector), :]
        copies = les_copies(k)
        copies[0].start()
        copies[1].start()
        u = [u_ref[c] for c in range(3)]
        edges = pick_edges(wide(les_pick, 16), u)
        les_st_send[k, 0] = edges[8:16]
        les_st_send[k, 1] = edges[0:8]
        copies[2].start()
        copies[3].start()
        if k == 0:
            send_margin(0, [caa_metric[c] for c in range(3)], 0)
            send_margin(1, [caa_out[c] for c in range(4)], 0)

        stacked = [u + [u[j] * u[i] for i in range(3)] for j in range(3)]
        along = right_apply(stacked[0], stream_mat[...])
        along = [along[i * rows : (i + 1) * rows] for i in range(6)]
        around = pieces(left_apply(wide(azimuth_mat, rows), stacked[1]), 6)
        across = pieces(left_apply(wide(radial_mat, rows), stacked[2]), 6)

        for copy in copies:
            copy.wait_recv()
        before, after = ghosts(les_st_recv, k)
        third = lax.broadcasted_iota(jnp.int32, before.shape, 0) >= 3
        before = before * jnp.where(third, before[0:1], 1.0)
        after = after * jnp.where(third, after[0:1], 1.0)
        fix = pieces(stream_fix(jnp.concatenate([before, after], axis=0), wide(stream_ghost, 32)), 6)
        along = [a + b for a, b in zip(along, fix)]
        rim = []
        for c in range(3):
            rim.append([les_az_recv[k, way, c * radial : (c + 1) * radial] for way in range(2)])
        rim = rim + [[rim[1][way] * rim[c][way] for way in range(2)] for c in range(3)]
        rim = jnp.concatenate([jnp.concatenate(pair, axis=0) for pair in rim], axis=1)
        fix = pieces(azimuth_fix(azimuth_ghost[...], rim), 6)
        around = [a + b for a, b in zip(around, fix)]
        slopes = [
            [les_metric[0] * along[i] for i in range(3)],
            [les_metric[1] * around[i] for i in range(3)],
            [les_metric[2] * across[i] for i in range(3)],
        ]
        first = slopes[1][2] - slopes[2][1]
        second = slopes[2][0] - slopes[0][2]
        third = slopes[0][1] - slopes[1][0]
        lamb = jnp.concatenate(
            [
                second * u[2] - third * u[1],
                third * u[0] - first * u[2],
                first * u[1] - second * u[0],
            ],
            axis=0,
        ).astype(BF16)
        chosen = product(lamb, chooser[...])
        depth = 3 * rows // groups
        group_lane = lax.broadcasted_iota(jnp.int32, (depth, stream), 1) // slot_lanes
        for d in range(n_gx):
            mine = chosen[:, d * stream : (d + 1) * stream]
            packed = mine[0:depth]
            for g in range(1, groups):
                packed = jnp.where(group_lane == g, mine[g * depth : (g + 1) * depth], packed)
            lamb_send[k, d] = packed.astype(BF16)
        for d in partners:
            lamb_copy(k, d).start()
        lamb_recv[k, gx] = lamb_send[k, gx]

        for i in range(3):
            change = les_metric[0] * along[3 + i] + u[0] * slopes[0][i]
            change += les_metric[1] * around[3 + i] + u[1] * slopes[1][i]
            change += les_metric[2] * across[3 + i] + u[2] * slopes[2][i]
            les_out[i] = u[i] - (0.5 * les_step) * change

    def substep(k, fresh):
        w = [caa_out[c] for c in range(4)]
        m = margin[...]
        for way, at in ((0, sector - 1), (1, 0)):
            ring = pl.ds(at, radial, stride=sector)
            caa_az_send[k, way, 0:radial] = caa_out[0, ring, :]
            caa_az_send[k, way, radial : 2 * radial] = caa_out[2, ring, :]
            caa_az_send[k, way, 2 * radial : 3 * radial] = swap_azimuth(margin[ring, :])
        copies = caa_copies(k)
        for copy in copies:
            copy.start()

        high, low = split(jnp.concatenate(w, axis=0))
        m_high, m_low = split(m)
        along = product(jnp.concatenate([high, low, high], axis=1), stream_mat[...])
        table = wide(inner, rows)
        fix = product(jnp.concatenate([m_high, m_low], axis=1), jnp.concatenate([table, table], axis=0))
        along = [caa_metric[0] * (along[i * rows : (i + 1) * rows] + b) for i, b in enumerate(pieces(fix, 4))]
        parts = [m_high, m_low, m_high]
        for c in range(4):
            parts += [high[c * rows : (c + 1) * rows], low[c * rows : (c + 1) * rows]]
        m_along = product(jnp.concatenate(parts, axis=1), margin_mat[...])
        around = pieces(left_apply(wide(azimuth_mat, rows), [w[0], w[2], swap_azimuth(m)]), 3)
        across = pieces(left_apply(wide(radial_mat, rows), [w[0], w[3], swap_radial(m)]), 3)

        for copy in copies:
            copy.wait_recv()
        rim = [
            jnp.concatenate([caa_az_recv[k, way, c * radial : (c + 1) * radial] for way in range(2)], axis=0)
            for c in range(3)
        ]
        fix = pieces(azimuth_fix(azimuth_ghost[...], jnp.concatenate(rim, axis=1)), 3)
        around = [a + b for a, b in zip(around, fix)]
        rates = [
            mach_number * along[0] + along[1] + caa_metric[1] * around[1] + caa_metric[2] * across[1],
            mach_number * along[1] + along[0] - source[0:rows],
            mach_number * along[2] + caa_metric[1] * around[0] - source[rows : 2 * rows],
            mach_number * along[3] + caa_metric[2] * across[0] - source[2 * rows : 3 * rows],
        ]
        for c in range(4):
            caa_out[c] = w[c] - caa_step * rates[c]
        if fresh is not None:
            margin_source[...] = take_margin(fresh)
        rate = margin_metric[0] * m_along + margin_metric[1] * around[2] + margin_metric[2] * across[2]
        margin[...] = m - caa_step * (rate - margin_source[...])

    def later_substep(k, carry):
        substep(k, None)
        return carry

    for k in range(LES_STEPS):
        if k > 0:
            send_margin(1 + 2 * k, [caa_out[c] for c in range(4)], 0)
        for d in partners:
            lamb_arrival(k, d).wait_recv()
        depth = 3 * rows // groups
        group_lane = lax.broadcasted_iota(jnp.int32, (depth, stream), 1) // slot_lanes
        for g in range(groups):
            got = [
                jnp.where(group_lane == g, lamb_recv[k, d].astype(F32), 0.0).astype(BF16) for d in range(n_gx)
            ]
            source[g * depth : (g + 1) * depth, :] = product(jnp.concatenate(got, axis=1), weights[...])
        send_margin(2 + 2 * k, [source[c * rows : (c + 1) * rows, :] for c in range(3)], 1)
        if k == 0:
            table = wide(spread, rows)
            spread_metric = pieces(product(take_margin(0).astype(BF16), table), 3)
            for c in range(3):
                margin_metric[c] = spread_metric[c]
        margin[...] = take_margin(1 + 2 * k)
        substep(k * CAA_SUB, 2 + 2 * k)
        lax.fori_loop(k * CAA_SUB + 1, (k + 1) * CAA_SUB, later_substep, 0)

    def drain_caa(k, carry):
        for copy in caa_copies(k):
            copy.wait_send()
        return carry

    lax.fori_loop(0, LES_STEPS * CAA_SUB, drain_caa, 0)
    for i in range(1 + 2 * LES_STEPS):
        for copy in margin_copies(i):
            copy.wait_send()
    for k in range(LES_STEPS):
        for copy in les_copies(k):
            copy.wait_send()
        for d in partners:
            lamb_copy(k, d).wait_send()


def hand_over(les_from, caa_from, les_to, caa_to, les_held, caa_held, sems):
    chains = ((les_from, les_held, les_to), (caa_from, caa_held, caa_to))
    loads = [pltpu.make_async_copy(a, b, sems.at[i]) for i, (a, b, _) in enumerate(chains)]
    stores = [pltpu.make_async_copy(b, c, sems.at[2 + i]) for i, (_, b, c) in enumerate(chains)]
    for load in loads:
        load.start()
    for load, store in zip(loads, stores):
        load.wait()
        store.start()
    for store in stores:
        store.wait()


def solution(mesh):
    n_sec, n_gx, n_az = mesh.shape["sec"], mesh.shape["gx"], mesh.shape["az"]

    def body(les_velocity, les_metric, caa_state, caa_metric, intersection_refs, offsets, send_list):
        radial, sector, stream = les_velocity.shape[1:]
        cap = send_list.shape[2]
        rows = radial * sector
        sizes = (n_sec, n_gx, n_az, radial, sector, stream, cap)
        consts = [jnp.asarray(t) for t in tables(radial, sector, stream)]
        flat = lambda x: x.reshape(x.shape[0], rows, stream)
        substeps = LES_STEPS * CAA_SUB
        depth = 3 * rows // (stream // (cap * block_nodes))
        vmem = pl.BlockSpec(memory_space=pltpu.VMEM)
        hbm = pl.BlockSpec(memory_space=pltpu.HBM)
        les_out, caa_out = pl.pallas_call(
            functools.partial(kernel, sizes),
            out_shape=(
                jax.ShapeDtypeStruct((3, rows, stream), F32),
                jax.ShapeDtypeStruct((4, rows, stream), F32),
            ),
            in_specs=[hbm] * (7 + len(consts)),
            out_specs=(vmem, vmem),
            scratch_shapes=[
                pltpu.VMEM((3, rows, stream), F32),
                pltpu.VMEM((3, rows, stream), F32),
                pltpu.VMEM((3, rows, stream), F32),
                pltpu.SMEM(intersection_refs.shape[::-1], jnp.int32),
                pltpu.SMEM(offsets.shape, jnp.int32),
                pltpu.SMEM(send_list.shape, jnp.int32),
            ]
            + [pltpu.VMEM(t.shape, BF16) for t in consts]
            + [
                pltpu.SemaphoreType.DMA((7 + len(consts),)),
                pltpu.VMEM((3 * rows, stream), F32),
                pltpu.VMEM((n_gx * stream, stream), BF16),
                pltpu.VMEM((rows, n_gx * stream), BF16),
                pltpu.VMEM((LES_STEPS, 2, 3 * radial, stream), F32),
                pltpu.VMEM((LES_STEPS, 2, 3 * radial, stream), F32),
                pltpu.VMEM((LES_STEPS, 2, 8, rows), F32),
                pltpu.VMEM((LES_STEPS, 2, 8, rows), F32),
                pltpu.VMEM((substeps, 2, 3 * radial, stream), F32),
                pltpu.VMEM((substeps, 2, 3 * radial, stream), F32),
                pltpu.VMEM((1 + 2 * LES_STEPS, rows, stream), BF16),
                pltpu.VMEM((1 + 2 * LES_STEPS, 2, rows, stream), BF16),
                pltpu.VMEM((rows, stream), F32),
                pltpu.VMEM((3, rows, stream), F32),
                pltpu.VMEM((rows, stream), F32),
                pltpu.VMEM((LES_STEPS, n_gx, depth, stream), BF16),
                pltpu.VMEM((LES_STEPS, n_gx, depth, stream), BF16),
                pltpu.SemaphoreType.DMA((LES_STEPS, 4, 2)),
                pltpu.SemaphoreType.DMA((substeps, 2, 2)),
                pltpu.SemaphoreType.DMA((1 + 2 * LES_STEPS, 2, 2)),
                pltpu.SemaphoreType.DMA((LES_STEPS, n_gx)),
                pltpu.SemaphoreType.DMA((LES_STEPS, n_gx)),
            ],
            compiler_params=pltpu.CompilerParams(
                collective_id=0, has_side_effects=True, vmem_limit_bytes=63 * 2**20
            ),
        )(
            flat(les_velocity), flat(les_metric), flat(caa_state), flat(caa_metric),
            intersection_refs.T, offsets, send_list, *consts,
        )
        shapes = [(3, rows, stream), (4, rows, stream)]
        les_out, caa_out = pl.pallas_call(
            hand_over,
            out_shape=tuple(jax.ShapeDtypeStruct(shape, F32) for shape in shapes),
            in_specs=[hbm] * 2,
            out_specs=(hbm, hbm),
            scratch_shapes=[pltpu.VMEM(shape, F32) for shape in shapes] + [pltpu.SemaphoreType.DMA((4,))],
            compiler_params=pltpu.CompilerParams(vmem_limit_bytes=63 * 2**20),
        )(les_out, caa_out)
        return les_out.reshape(les_velocity.shape), caa_out.reshape(caa_state.shape)

    in_specs = (
        P(None, None, "az", ("sec", "gx")),
        P(None, None, "az", ("sec", "gx")),
        P(None, None, "az", ("sec", "gx")),
        P(None, None, "az", ("sec", "gx")),
        P(("sec", "gx"), None),
        P(("sec", "gx")),
        P(),
    )
    out_specs = (P(None, None, "az", ("sec", "gx")), P(None, None, "az", ("sec", "gx")))
    return jax.shard_map(body, mesh=mesh, in_specs=in_specs, out_specs=out_specs, check_vma=False)
```

```python
import functools

import jax
import jax.numpy as jnp
import numpy as np
from jax import lax
from jax.experimental import pallas as pl
from jax.experimental.pallas import tpu as pltpu
from jax.sharding import PartitionSpec as P

LES_STEPS = 2
CAA_SUB = 4

les_step = 0.02
caa_step = 0.01
mach_number = 0.5
block_nodes = 8
margin_nodes = 16
MESH = pl.DeviceIdType.MESH
F32 = jnp.float32
BF16 = jnp.bfloat16


def slope_table():
    points = np.array([-1.0, -(0.2**0.5), 0.2**0.5, 1.0])
    identity = np.eye(4)
    differences = points[:, None] - points[None, :] + identity
    inverse_weights = 1.0 / np.prod(differences, axis=1)
    slope_matrix = inverse_weights[None, :] / inverse_weights[:, None] / differences
    slope_matrix = slope_matrix * (1.0 - identity)
    return slope_matrix - identity * slope_matrix.sum(axis=1)[:, None]


def line_matrix(length):
    slope_matrix = slope_table()
    result = np.zeros((length + 2, length))
    for element in range(length // 4):
        at = 4 * element
        result[1 + at : 5 + at, at : at + 4] += slope_matrix.T
        result[at + 1, at] += 3.0
        result[at, at] -= 3.0
        result[at + 5, at + 3] += 3.0
        result[at + 4, at + 3] -= 3.0
    return result[1:-1].T


def halves(matrix):
    high = matrix.astype(np.float32).astype(BF16)
    low = (matrix - high.astype(np.float64)).astype(np.float32).astype(BF16)
    return high, low


def tables(radial, sector, stream):
    rows = radial * sector
    high, low = halves(line_matrix(stream).T)
    stream_mat = np.concatenate([high, high, low], axis=0)
    high, low = halves(np.kron(np.eye(radial), line_matrix(sector)))
    azimuth_mat = np.concatenate([high, high, low], axis=1)
    high, low = halves(np.kron(line_matrix(radial), np.eye(sector)))
    radial_mat = np.concatenate([high, high, low], axis=1)
    ghost = np.zeros((rows, 2 * radial))
    for r in range(radial):
        ghost[r * sector, r] = -3.0
        ghost[r * sector + sector - 1, radial + r] = 3.0
    azimuth_ghost = np.concatenate([ghost, ghost], axis=1).astype(BF16)
    ghost = np.zeros((16, 6 * stream))
    for c in range(6):
        ghost[c, c * stream] = -3.0
        ghost[8 + c, c * stream + stream - 1] = 3.0
    stream_ghost = np.concatenate([ghost, ghost], axis=0).astype(BF16)
    pick = np.zeros((16, 3 * stream))
    for c in range(6):
        pick[c, (c % 3) * stream] = 1.0
        pick[8 + c, (c % 3) * stream + stream - 1] = 1.0
    les_pick = np.concatenate([pick, pick], axis=1).astype(BF16)
    m = margin_nodes
    inner = np.zeros((stream, 4 * stream))
    mix = mach_number * np.eye(4)
    mix[1, 0] = mix[0, 1] = 1.0
    joint = np.zeros((4, stream, stream))
    spread = np.zeros((stream, 3 * stream))
    for c in range(4):
        inner[2 * m * c + m - 1, c * stream] = -3.0
        inner[2 * m * c + m, c * stream + stream - 1] = 3.0
        for o in range(4):
            joint[c, 0, 2 * m * o + m - 1] = 3.0 * mix[c, o]
            joint[c, stream - 1, 2 * m * o + m] = -3.0 * mix[c, o]
            if c < 3:
                for t in range(2 * m):
                    spread[2 * m * c + t, c * stream + 2 * m * o + t] = 1.0
    high, low = halves(np.kron(mix, np.kron(np.eye(2), line_matrix(m).T)))
    joint = [joint[c // 2].astype(BF16) for c in range(8)]
    margin_mat = np.concatenate([high, high, low] + joint, axis=0)
    columns = [azimuth_mat, radial_mat, stream_ghost, les_pick, inner.astype(BF16), spread.astype(BF16)]
    return [stream_mat, azimuth_ghost, margin_mat] + [tall(t, stream) for t in columns]


def tall(table, width):
    return np.concatenate([table[:, i : i + width] for i in range(0, table.shape[1], width)], axis=0)


def wide(ref, height, count=None):
    count = ref.shape[0] // height if count is None else count
    return jnp.concatenate([ref[i * height : (i + 1) * height, :] for i in range(count)], axis=1)


def split(value):
    high = value.astype(BF16)
    return high, (value - high.astype(F32)).astype(BF16)


def product(left, right):
    return jnp.dot(left, right, preferred_element_type=F32)


def right_apply(fields, matrix):
    high, low = split(jnp.concatenate(fields, axis=0))
    return product(jnp.concatenate([high, low, high], axis=1), matrix)


def left_apply(matrix, fields):
    high, low = split(jnp.concatenate(fields, axis=1))
    return product(matrix, jnp.concatenate([high, low, high], axis=0))


def pick_edges(pick, fields):
    high, low = split(jnp.concatenate(fields, axis=1))
    return lax.dot_general(
        pick, jnp.concatenate([high, low], axis=1), (((1,), (1,)), ((), ())), preferred_element_type=F32
    )


def stream_fix(rim, ghost):
    high, low = split(rim)
    both = jnp.concatenate([high.astype(F32), low.astype(F32)], axis=0)
    return product(both.T.astype(BF16), ghost)


def azimuth_fix(ghost, rim):
    high, low = split(rim)
    return product(ghost, jnp.concatenate([high, low], axis=0))


def kernel(
    sizes,
    les_hbm, les_metric_hbm, caa_hbm, caa_metric_hbm, refs_hbm, offsets_hbm, send_list_hbm,
    stream_mat_hbm, azimuth_ghost_hbm, margin_mat_hbm,
    azimuth_mat_hbm, radial_mat_hbm, stream_ghost_hbm, les_pick_hbm, inner_hbm, spread_hbm,
    les_out, caa_out,
    les_in, les_metric, caa_metric, refs, offsets, send_list,
    stream_mat, azimuth_ghost, margin_mat, azimuth_mat, radial_mat, stream_ghost, les_pick, inner, spread,
    load_sems,
    source, weights, chooser,
    les_az_send, les_az_recv, les_st_send, les_st_recv,
    caa_az_send, caa_az_recv, margin_send, margin_recv, margin, margin_metric, margin_source,
    lamb_send, lamb_recv,
    les_sems, caa_sems, margin_sems, lamb_send_sem, lamb_recv_sem,
):
    n_sec, n_gx, n_az, radial, sector, stream, cap = sizes
    rows = radial * sector
    sec, gx, az = lax.axis_index("sec"), lax.axis_index("gx"), lax.axis_index("az")
    slabs = n_sec * n_gx
    slab = sec * n_gx + gx
    up, down = lax.rem(slab + slabs - 1, slabs), lax.rem(slab + 1, slabs)
    up_id = {"sec": up // n_gx, "gx": lax.rem(up, n_gx), "az": az}
    down_id = {"sec": down // n_gx, "gx": lax.rem(down, n_gx), "az": az}
    below_id = {"sec": sec, "gx": gx, "az": lax.rem(az + n_az - 1, n_az)}
    above_id = {"sec": sec, "gx": gx, "az": lax.rem(az + 1, n_az)}
    partners = [lax.rem(gx + k, n_gx) for k in range(1, n_gx)]

    barrier = pltpu.get_barrier_semaphore()
    for device in [up_id, down_id, below_id, above_id] + [{"sec": sec, "gx": d, "az": az} for d in partners]:
        pl.semaphore_signal(barrier, inc=1, device_id=device, device_id_type=MESH)

    loads = [
        pltpu.make_async_copy(src, dst, load_sems.at[i])
        for i, (src, dst) in enumerate(
            [
                (refs_hbm, refs), (offsets_hbm, offsets), (send_list_hbm, send_list),
                (les_hbm, les_in), (les_pick_hbm, les_pick),
                (stream_mat_hbm, stream_mat), (azimuth_mat_hbm, azimuth_mat), (radial_mat_hbm, radial_mat),
                (azimuth_ghost_hbm, azimuth_ghost), (stream_ghost_hbm, stream_ghost),
                (les_metric_hbm, les_metric), (caa_hbm, caa_out), (margin_mat_hbm, margin_mat), (inner_hbm, inner), (spread_hbm, spread),
                (caa_metric_hbm, caa_metric),
            ]
        )
    ]
    for load in loads:
        load.start()
    for load in loads[0:3]:
        load.wait()

    lane = lax.broadcasted_iota(jnp.int32, (rows, stream), 1)
    row = lax.broadcasted_iota(jnp.int32, (rows, stream), 0)
    slot_lanes = cap * block_nodes
    groups = stream // slot_lanes
    slot_of_lane = lax.rem(lane, slot_lanes) // block_nodes
    slot_of_row = lax.rem(row, slot_lanes) // block_nodes
    node_of_lane = lax.rem(lane, block_nodes)
    same_node = lax.rem(row, block_nodes) == node_of_lane
    one_lane = lane[0:1]
    block_of_lane = one_lane // block_nodes
    lead = jnp.zeros((1, stream), jnp.int32)
    trail = jnp.zeros((1, stream), jnp.int32)
    part = jnp.zeros((1, stream), jnp.int32)
    for j in range(stream // block_nodes):
        here = block_of_lane == j
        lead = jnp.where(here, refs[0, j] * cap + refs[1, j], lead)
        trail = jnp.where(here, refs[2, j] * cap + refs[3, j], trail)
        part = jnp.where(here, offsets[j], part)
    trail_weight = part.astype(F32) / 8.0
    lead_weight = 1.0 - trail_weight
    for d in range(n_gx):
        code = slot_of_row + d * cap
        weight = jnp.where(code == lead, lead_weight, 0.0) + jnp.where(code == trail, trail_weight, 0.0)
        weights[d * stream : (d + 1) * stream, :] = jnp.where(same_node, weight, 0.0).astype(BF16)
        taken = jnp.zeros((1, stream), jnp.int32)
        for c in range(cap):
            taken = jnp.where(slot_of_lane[0:1] == c, send_list[slab, d, c], taken)
        wanted = taken * block_nodes + node_of_lane[0:1]
        chooser[:, d * stream : (d + 1) * stream] = jnp.where(row == wanted, 1.0, 0.0).astype(BF16)

    def pair(sems, k, first, send, recv, devices):
        return [
            pltpu.make_async_remote_copy(
                src_ref=send.at[k, way], dst_ref=recv.at[k, way],
                send_sem=sems.at[k, first + way, 0], recv_sem=sems.at[k, first + way, 1],
                device_id=devices[way], device_id_type=MESH,
            )
            for way in range(2)
        ]

    def les_copies(k):
        copies = pair(les_sems, k, 0, les_az_send, les_az_recv, (above_id, below_id))
        return copies + pair(les_sems, k, 2, les_st_send, les_st_recv, (down_id, up_id))

    def caa_copies(k):
        return pair(caa_sems, k, 0, caa_az_send, caa_az_recv, (above_id, below_id))

    def margin_copies(i):
        return [
            pltpu.make_async_remote_copy(
                src_ref=margin_send.at[i], dst_ref=margin_recv.at[i, way],
                send_sem=margin_sems.at[i, way, 0], recv_sem=margin_sems.at[i, way, 1],
                device_id=(down_id, up_id)[way], device_id_type=MESH,
            )
            for way in range(2)
        ]

    width = 2 * margin_nodes
    group = lane // width

    def send_margin(i, fields, first):
        packed = jnp.zeros((rows, stream), F32)
        for c, field in enumerate(fields, first):
            packed = jnp.where(group == c, pltpu.roll(field, width * c + margin_nodes, 1), packed)
        margin_send[i] = packed.astype(BF16)
        for copy in margin_copies(i):
            copy.start()

    def take_margin(i):
        for copy in margin_copies(i):
            copy.wait_recv()
        before = jnp.where(slab > 0, margin_recv[i, 0].astype(F32), 0.0)
        after = jnp.where(slab < slabs - 1, margin_recv[i, 1].astype(F32), 0.0)
        return jnp.where(lax.rem(lane, width) < margin_nodes, before, after)

    def swap_azimuth(value):
        at = lax.broadcasted_iota(jnp.int32, value.shape, 1) // width
        return jnp.where(lax.rem(at, 2) == 0, pltpu.roll(value, 2 * width, 1), 0.0)

    def swap_radial(value):
        return jnp.where(
            group == 0, pltpu.roll(value, width, 1), jnp.where(group == 3, pltpu.roll(value, 3 * width, 1), 0.0)
        )

    def lamb_copy(k, d):
        return pltpu.make_async_remote_copy(
            src_ref=lamb_send.at[k, d], dst_ref=lamb_recv.at[k, gx],
            send_sem=lamb_send_sem.at[k, d], recv_sem=lamb_recv_sem.at[k, gx],
            device_id={"sec": sec, "gx": d, "az": az}, device_id_type=MESH,
        )

    def lamb_arrival(k, d):
        return pltpu.make_async_remote_copy(
            src_ref=lamb_send.at[k, d], dst_ref=lamb_recv.at[k, d],
            send_sem=lamb_send_sem.at[k, d], recv_sem=lamb_recv_sem.at[k, d],
            device_id={"sec": sec, "gx": d, "az": az}, device_id_type=MESH,
        )

    def ghosts(recv, k):
        before = jnp.where(slab > 0, recv[k, 0], 0.0)
        after = jnp.where(slab < slabs - 1, recv[k, 1], 0.0)
        return before, after

    def pieces(value, count):
        return [value[:, i * stream : (i + 1) * stream] for i in range(count)]

    for load in loads[3:]:
        load.wait()
    pl.semaphore_wait(barrier, 4 + len(partners))

    for k in range(LES_STEPS):
        u_ref = les_in if k == 0 else les_out
        for c in range(3):
            les_az_send[k, 0, c * radial : (c + 1) * radial] = u_ref[c, pl.ds(sector - 1, radial, stride=sector), :]
            les_az_send[k, 1, c * radial : (c + 1) * radial] = u_ref[c, pl.ds(0, radial, stride=sector), :]
        copies = les_copies(k)
        copies[0].start()
        copies[1].start()
        u = [u_ref[c] for c in range(3)]
        edges = pick_edges(wide(les_pick, 16), u)
        les_st_send[k, 0] = edges[8:16]
        les_st_send[k, 1] = edges[0:8]
        copies[2].start()
        copies[3].start()
        if k == 0:
            send_margin(0, [caa_metric[c] for c in range(3)], 0)
            send_margin(1, [caa_out[c] for c in range(4)], 0)

        stacked = [u + [u[j] * u[i] for i in range(3)] for j in range(3)]
        along = right_apply(stacked[0], stream_mat[...])
        along = [along[i * rows : (i + 1) * rows] for i in range(6)]
        around = pieces(left_apply(wide(azimuth_mat, rows), stacked[1]), 6)
        across = pieces(left_apply(wide(radial_mat, rows), stacked[2]), 6)

        for copy in copies:
            copy.wait_recv()
        before, after = ghosts(les_st_recv, k)
        third = lax.broadcasted_iota(jnp.int32, before.shape, 0) >= 3
        before = before * jnp.where(third, before[0:1], 1.0)
        after = after * jnp.where(third, after[0:1], 1.0)
        fix = pieces(stream_fix(jnp.concatenate([before, after], axis=0), wide(stream_ghost, 32)), 6)
        along = [a + b for a, b in zip(along, fix)]
        rim = []
        for c in range(3):
            rim.append([les_az_recv[k, way, c * radial : (c + 1) * radial] for way in range(2)])
        rim = rim + [[rim[1][way] * rim[c][way] for way in range(2)] for c in range(3)]
        rim = jnp.concatenate([jnp.concatenate(pair, axis=0) for pair in rim], axis=1)
        fix = pieces(azimuth_fix(azimuth_ghost[...], rim), 6)
        around = [a + b for a, b in zip(around, fix)]
        slopes = [
            [les_metric[0] * along[i] for i in range(3)],
            [les_metric[1] * around[i] for i in range(3)],
            [les_metric[2] * across[i] for i in range(3)],
        ]
        first = slopes[1][2] - slopes[2][1]
        second = slopes[2][0] - slopes[0][2]
        third = slopes[0][1] - slopes[1][0]
        lamb = jnp.concatenate(
            [
                second * u[2] - third * u[1],
                third * u[0] - first * u[2],
                first * u[1] - second * u[0],
            ],
            axis=0,
        ).astype(BF16)
        chosen = product(lamb, chooser[...])
        depth = 3 * rows // groups
        group_lane = lax.broadcasted_iota(jnp.int32, (depth, stream), 1) // slot_lanes
        for d in range(n_gx):
            mine = chosen[:, d * stream : (d + 1) * stream]
            packed = mine[0:depth]
            for g in range(1, groups):
                packed = jnp.where(group_lane == g, mine[g * depth : (g + 1) * depth], packed)
            lamb_send[k, d] = packed.astype(BF16)
        for d in partners:
            lamb_copy(k, d).start()
        lamb_recv[k, gx] = lamb_send[k, gx]

        for i in range(3):
            change = les_metric[0] * along[3 + i] + u[0] * slopes[0][i]
            change += les_metric[1] * around[3 + i] + u[1] * slopes[1][i]
            change += les_metric[2] * across[3 + i] + u[2] * slopes[2][i]
            les_out[i] = u[i] - (0.5 * les_step) * change

    rings = (pl.ds(sector - 1, radial, stride=sector), pl.ds(0, radial, stride=sector))

    def send_rows(k, way, p, v, m):
        caa_az_send[k, way, 0:radial] = p
        caa_az_send[k, way, radial : 2 * radial] = v
        caa_az_send[k, way, 2 * radial : 3 * radial] = swap_azimuth(m)
        caa_copies(k)[way].start()

    def substep(k, fresh, last):
        w = [caa_out[c] for c in range(4)]
        m = margin[...]
        high, low = split(jnp.concatenate(w, axis=0))
        m_high, m_low = split(m)
        along = product(jnp.concatenate([high, low, high], axis=1), stream_mat[...])
        table = wide(inner, rows)
        fix = product(jnp.concatenate([m_high, m_low], axis=1), jnp.concatenate([table, table], axis=0))
        along = [caa_metric[0] * (along[i * rows : (i + 1) * rows] + b) for i, b in enumerate(pieces(fix, 4))]
        parts = [m_high, m_low, m_high]
        w_high = [high[c * rows : (c + 1) * rows] for c in range(4)]
        w_low = [low[c * rows : (c + 1) * rows] for c in range(4)]
        for c in range(4):
            parts += [w_high[c], w_low[c]]
        m_along = product(jnp.concatenate(parts, axis=1), margin_mat[...])

        def across_rows(matrix, c, swapped):
            s_high, s_low = split(swapped)
            top = jnp.concatenate([w_high[0], w_high[c], s_high], axis=1)
            under = jnp.concatenate([w_low[0], w_low[c], s_low], axis=1)
            return pieces(product(wide(matrix, rows), jnp.concatenate([top, under, top], axis=0)), 3)

        around = across_rows(azimuth_mat, 2, swap_azimuth(m))
        across = across_rows(radial_mat, 3, swap_radial(m))
        rates = [
            mach_number * along[0] + along[1] + caa_metric[1] * around[1] + caa_metric[2] * across[1],
            mach_number * along[1] + along[0] - source[0:rows],
            mach_number * along[2] + caa_metric[1] * around[0] - source[rows : 2 * rows],
            mach_number * along[3] + caa_metric[2] * across[0] - source[2 * rows : 3 * rows],
        ]
        for c in range(4):
            caa_out[c] = w[c] - caa_step * rates[c]
        if fresh is not None:
            margin_source[...] = take_margin(fresh)
        rate = margin_metric[0] * m_along + margin_metric[1] * around[2] + margin_metric[2] * across[2]
        margin[...] = m - caa_step * (rate - margin_source[...])

        copies = caa_copies(k)
        for way in range(2):
            copies[way].wait_recv()
            ring = rings[1 - way]
            scale = (3.0 * caa_step) * (1.0 - 2.0 * way)
            halo = [caa_az_recv[k, way, c * radial : (c + 1) * radial] for c in range(3)]
            p = caa_out[0, ring, :] + scale * caa_metric[1, ring, :] * halo[1]
            v = caa_out[2, ring, :] + scale * caa_metric[1, ring, :] * halo[0]
            edge = margin[ring, :] + scale * margin_metric[1, ring, :] * halo[2]
            caa_out[0, ring, :] = p
            caa_out[2, ring, :] = v
            margin[ring, :] = edge
            if not last:
                send_rows(k + 1, 1 - way, p, v, edge)

    def later_substep(k, carry):
        substep(k, None, False)
        return carry

    for k in range(LES_STEPS):
        if k > 0:
            send_margin(1 + 2 * k, [caa_out[c] for c in range(4)], 0)
        for d in partners:
            lamb_arrival(k, d).wait_recv()
        depth = 3 * rows // groups
        group_lane = lax.broadcasted_iota(jnp.int32, (depth, stream), 1) // slot_lanes
        for g in range(groups):
            got = [
                jnp.where(group_lane == g, lamb_recv[k, d].astype(F32), 0.0).astype(BF16) for d in range(n_gx)
            ]
            source[g * depth : (g + 1) * depth, :] = product(jnp.concatenate(got, axis=1), weights[...])
        send_margin(2 + 2 * k, [source[c * rows : (c + 1) * rows, :] for c in range(3)], 1)
        if k == 0:
            table = wide(spread, rows)
            spread_metric = pieces(product(take_margin(0).astype(BF16), table), 3)
            for c in range(3):
                margin_metric[c] = spread_metric[c]
        margin[...] = take_margin(1 + 2 * k)
        begin = k * CAA_SUB
        for way in range(2):
            ring = rings[way]
            send_rows(begin, way, caa_out[0, ring, :], caa_out[2, ring, :], margin[ring, :])
        substep(begin, 2 + 2 * k, False)
        lax.fori_loop(begin + 1, begin + CAA_SUB - 1, later_substep, 0)
        substep(begin + CAA_SUB - 1, None, True)

    def drain_caa(k, carry):
        for copy in caa_copies(k):
            copy.wait_send()
        return carry

    lax.fori_loop(0, LES_STEPS * CAA_SUB, drain_caa, 0)
    for i in range(1 + 2 * LES_STEPS):
        for copy in margin_copies(i):
            copy.wait_send()
    for k in range(LES_STEPS):
        for copy in les_copies(k):
            copy.wait_send()
        for d in partners:
            lamb_copy(k, d).wait_send()


def hand_over(les_from, caa_from, les_to, caa_to, les_held, caa_held, sems):
    chains = ((les_from, les_held, les_to), (caa_from, caa_held, caa_to))
    loads = [pltpu.make_async_copy(a, b, sems.at[i]) for i, (a, b, _) in enumerate(chains)]
    stores = [pltpu.make_async_copy(b, c, sems.at[2 + i]) for i, (_, b, c) in enumerate(chains)]
    for load in loads:
        load.start()
    for load, store in zip(loads, stores):
        load.wait()
        store.start()
    for store in stores:
        store.wait()


def solution(mesh):
    n_sec, n_gx, n_az = mesh.shape["sec"], mesh.shape["gx"], mesh.shape["az"]

    def body(les_velocity, les_metric, caa_state, caa_metric, intersection_refs, offsets, send_list):
        radial, sector, stream = les_velocity.shape[1:]
        cap = send_list.shape[2]
        rows = radial * sector
        sizes = (n_sec, n_gx, n_az, radial, sector, stream, cap)
        consts = [jnp.asarray(t) for t in tables(radial, sector, stream)]
        flat = lambda x: x.reshape(x.shape[0], rows, stream)
        substeps = LES_STEPS * CAA_SUB
        depth = 3 * rows // (stream // (cap * block_nodes))
        vmem = pl.BlockSpec(memory_space=pltpu.VMEM)
        hbm = pl.BlockSpec(memory_space=pltpu.HBM)
        les_out, caa_out = pl.pallas_call(
            functools.partial(kernel, sizes),
            out_shape=(
                jax.ShapeDtypeStruct((3, rows, stream), F32),
                jax.ShapeDtypeStruct((4, rows, stream), F32),
            ),
            in_specs=[hbm] * (7 + len(consts)),
            out_specs=(vmem, vmem),
            scratch_shapes=[
                pltpu.VMEM((3, rows, stream), F32),
                pltpu.VMEM((3, rows, stream), F32),
                pltpu.VMEM((3, rows, stream), F32),
                pltpu.SMEM(intersection_refs.shape[::-1], jnp.int32),
                pltpu.SMEM(offsets.shape, jnp.int32),
                pltpu.SMEM(send_list.shape, jnp.int32),
            ]
            + [pltpu.VMEM(t.shape, BF16) for t in consts]
            + [
                pltpu.SemaphoreType.DMA((7 + len(consts),)),
                pltpu.VMEM((3 * rows, stream), F32),
                pltpu.VMEM((n_gx * stream, stream), BF16),
                pltpu.VMEM((rows, n_gx * stream), BF16),
                pltpu.VMEM((LES_STEPS, 2, 3 * radial, stream), F32),
                pltpu.VMEM((LES_STEPS, 2, 3 * radial, stream), F32),
                pltpu.VMEM((LES_STEPS, 2, 8, rows), F32),
                pltpu.VMEM((LES_STEPS, 2, 8, rows), F32),
                pltpu.VMEM((substeps, 2, 3 * radial, stream), F32),
                pltpu.VMEM((substeps, 2, 3 * radial, stream), F32),
                pltpu.VMEM((1 + 2 * LES_STEPS, rows, stream), BF16),
                pltpu.VMEM((1 + 2 * LES_STEPS, 2, rows, stream), BF16),
                pltpu.VMEM((rows, stream), F32),
                pltpu.VMEM((3, rows, stream), F32),
                pltpu.VMEM((rows, stream), F32),
                pltpu.VMEM((LES_STEPS, n_gx, depth, stream), BF16),
                pltpu.VMEM((LES_STEPS, n_gx, depth, stream), BF16),
                pltpu.SemaphoreType.DMA((LES_STEPS, 4, 2)),
                pltpu.SemaphoreType.DMA((substeps, 2, 2)),
                pltpu.SemaphoreType.DMA((1 + 2 * LES_STEPS, 2, 2)),
                pltpu.SemaphoreType.DMA((LES_STEPS, n_gx)),
                pltpu.SemaphoreType.DMA((LES_STEPS, n_gx)),
            ],
            compiler_params=pltpu.CompilerParams(
                collective_id=0, has_side_effects=True, vmem_limit_bytes=63 * 2**20
            ),
        )(
            flat(les_velocity), flat(les_metric), flat(caa_state), flat(caa_metric),
            intersection_refs.T, offsets, send_list, *consts,
        )
        shapes = [(3, rows, stream), (4, rows, stream)]
        les_out, caa_out = pl.pallas_call(
            hand_over,
            out_shape=tuple(jax.ShapeDtypeStruct(shape, F32) for shape in shapes),
            in_specs=[hbm] * 2,
            out_specs=(hbm, hbm),
            scratch_shapes=[pltpu.VMEM(shape, F32) for shape in shapes] + [pltpu.SemaphoreType.DMA((4,))],
            compiler_params=pltpu.CompilerParams(vmem_limit_bytes=63 * 2**20),
        )(les_out, caa_out)
        return les_out.reshape(les_velocity.shape), caa_out.reshape(caa_state.shape)

    in_specs = (
        P(None, None, "az", ("sec", "gx")),
        P(None, None, "az", ("sec", "gx")),
        P(None, None, "az", ("sec", "gx")),
        P(None, None, "az", ("sec", "gx")),
        P(("sec", "gx"), None),
        P(("sec", "gx")),
        P(),
    )
    out_specs = (P(None, None, "az", ("sec", "gx")), P(None, None, "az", ("sec", "gx")))
    return jax.shard_map(body, mesh=mesh, in_specs=in_specs, out_specs=out_specs, check_vma=False)
```

```python
import functools

import jax
import jax.numpy as jnp
import numpy as np
from jax import lax
from jax.experimental import pallas as pl
from jax.experimental.pallas import tpu as pltpu
from jax.sharding import PartitionSpec as P

LES_STEPS = 2
CAA_SUB = 4

les_step = 0.02
caa_step = 0.01
mach_number = 0.5
block_nodes = 8
margin_nodes = 16
MESH = pl.DeviceIdType.MESH
F32 = jnp.float32
BF16 = jnp.bfloat16


def slope_table():
    points = np.array([-1.0, -(0.2**0.5), 0.2**0.5, 1.0])
    identity = np.eye(4)
    differences = points[:, None] - points[None, :] + identity
    inverse_weights = 1.0 / np.prod(differences, axis=1)
    slope_matrix = inverse_weights[None, :] / inverse_weights[:, None] / differences
    slope_matrix = slope_matrix * (1.0 - identity)
    return slope_matrix - identity * slope_matrix.sum(axis=1)[:, None]


def line_matrix(length):
    slope_matrix = slope_table()
    result = np.zeros((length + 2, length))
    for element in range(length // 4):
        at = 4 * element
        result[1 + at : 5 + at, at : at + 4] += slope_matrix.T
        result[at + 1, at] += 3.0
        result[at, at] -= 3.0
        result[at + 5, at + 3] += 3.0
        result[at + 4, at + 3] -= 3.0
    return result[1:-1].T


def halves(matrix):
    high = matrix.astype(np.float32).astype(BF16)
    low = (matrix - high.astype(np.float64)).astype(np.float32).astype(BF16)
    return high, low


def tables(radial, sector, stream):
    rows = radial * sector
    high, low = halves(line_matrix(stream).T)
    stream_mat = np.concatenate([high, high, low], axis=0)
    high, low = halves(np.kron(np.eye(radial), line_matrix(sector)))
    azimuth_mat = np.concatenate([high, high, low], axis=1)
    ghost = np.zeros((rows, 2 * radial))
    for r in range(radial):
        ghost[r * sector, r] = -3.0
        ghost[r * sector + sector - 1, radial + r] = 3.0
    azimuth_ghost = np.concatenate([ghost, ghost], axis=1).astype(BF16)
    ghost = np.zeros((16, 6 * stream))
    for c in range(6):
        ghost[c, c * stream] = -3.0
        ghost[8 + c, c * stream + stream - 1] = 3.0
    stream_ghost = np.concatenate([ghost, ghost], axis=0).astype(BF16)
    pick = np.zeros((16, 3 * stream))
    for c in range(6):
        pick[c, (c % 3) * stream] = 1.0
        pick[8 + c, (c % 3) * stream + stream - 1] = 1.0
    les_pick = np.concatenate([pick, pick], axis=1).astype(BF16)
    m = margin_nodes
    inner = np.zeros((stream, 4 * stream))
    mix = mach_number * np.eye(4)
    mix[1, 0] = mix[0, 1] = 1.0
    joint = np.zeros((stream, stream))
    spread = np.zeros((stream, 3 * stream))
    for c in range(4):
        inner[2 * m * c + m - 1, c * stream] = -3.0
        inner[2 * m * c + m, c * stream + stream - 1] = 3.0
        for o in range(4):
            joint[0, 2 * m * o + m - 1] = 3.0
            joint[stream - 1, 2 * m * o + m] = -3.0
            if c < 3:
                for t in range(2 * m):
                    spread[2 * m * c + t, c * stream + 2 * m * o + t] = 1.0
    high, low = halves(np.kron(mix, np.kron(np.eye(2), line_matrix(m).T)))
    margin_mat = np.concatenate([high, low], axis=0)
    joint = joint.astype(BF16)
    joint = np.concatenate([joint, joint, 0 * joint], axis=0)
    columns = [azimuth_mat, stream_ghost, les_pick, inner.astype(BF16), spread.astype(BF16)]
    return [stream_mat, azimuth_ghost, margin_mat, joint] + [tall(t, stream) for t in columns]


def tall(table, width):
    return np.concatenate([table[:, i : i + width] for i in range(0, table.shape[1], width)], axis=0)


def wide(ref, height, count=None):
    count = ref.shape[0] // height if count is None else count
    return jnp.concatenate([ref[i * height : (i + 1) * height, :] for i in range(count)], axis=1)


def split(value):
    high = value.astype(BF16)
    return high, (value - high.astype(F32)).astype(BF16)


def product(left, right):
    return jnp.dot(left, right, preferred_element_type=F32)


def right_apply(fields, matrix):
    high, low = split(jnp.concatenate(fields, axis=0))
    return product(jnp.concatenate([high, low, high], axis=1), matrix)


def left_apply(matrix, fields):
    high, low = split(jnp.concatenate(fields, axis=1))
    return product(matrix, jnp.concatenate([high, low, high], axis=0))


def pick_edges(pick, fields):
    high, low = split(jnp.concatenate(fields, axis=1))
    return lax.dot_general(
        pick, jnp.concatenate([high, low], axis=1), (((1,), (1,)), ((), ())), preferred_element_type=F32
    )


def stream_fix(rim, ghost):
    high, low = split(rim)
    both = jnp.concatenate([high.astype(F32), low.astype(F32)], axis=0)
    return product(both.T.astype(BF16), ghost)


def azimuth_fix(ghost, rim):
    high, low = split(rim)
    return product(ghost, jnp.concatenate([high, low], axis=0))


def kernel(
    sizes,
    les_hbm, les_metric_hbm, caa_hbm, caa_metric_hbm, refs_hbm, offsets_hbm, send_list_hbm,
    stream_mat_hbm, azimuth_ghost_hbm, margin_mat_hbm, joint_hbm,
    azimuth_mat_hbm, stream_ghost_hbm, les_pick_hbm, inner_hbm, spread_hbm,
    les_out, caa_out,
    les_in, les_metric, caa_metric, refs, offsets, send_list,
    stream_mat, azimuth_ghost, margin_mat, joint, azimuth_mat, stream_ghost, les_pick, inner, spread,
    load_sems,
    source, weights, chooser,
    les_az_send, les_az_recv, les_st_send, les_st_recv,
    caa_az_send, caa_az_recv, margin_send, margin_recv, margin, margin_metric, margin_source,
    lamb_send, lamb_recv,
    les_sems, caa_sems, margin_sems, lamb_send_sem, lamb_recv_sem,
):
    n_sec, n_gx, n_az, radial, sector, stream, cap = sizes
    rows = radial * sector
    sec, gx, az = lax.axis_index("sec"), lax.axis_index("gx"), lax.axis_index("az")
    slabs = n_sec * n_gx
    slab = sec * n_gx + gx
    up, down = lax.rem(slab + slabs - 1, slabs), lax.rem(slab + 1, slabs)
    up_id = {"sec": up // n_gx, "gx": lax.rem(up, n_gx), "az": az}
    down_id = {"sec": down // n_gx, "gx": lax.rem(down, n_gx), "az": az}
    below_id = {"sec": sec, "gx": gx, "az": lax.rem(az + n_az - 1, n_az)}
    above_id = {"sec": sec, "gx": gx, "az": lax.rem(az + 1, n_az)}
    partners = [lax.rem(gx + k, n_gx) for k in range(1, n_gx)]

    barrier = pltpu.get_barrier_semaphore()
    for device in [up_id, down_id, below_id, above_id] + [{"sec": sec, "gx": d, "az": az} for d in partners]:
        pl.semaphore_signal(barrier, inc=1, device_id=device, device_id_type=MESH)

    loads = [
        pltpu.make_async_copy(src, dst, load_sems.at[i])
        for i, (src, dst) in enumerate(
            [
                (refs_hbm, refs), (offsets_hbm, offsets), (send_list_hbm, send_list),
                (les_hbm, les_in), (les_pick_hbm, les_pick),
                (stream_mat_hbm, stream_mat), (azimuth_mat_hbm, azimuth_mat), (joint_hbm, joint),
                (azimuth_ghost_hbm, azimuth_ghost), (stream_ghost_hbm, stream_ghost),
                (les_metric_hbm, les_metric), (caa_hbm, caa_out), (margin_mat_hbm, margin_mat), (inner_hbm, inner), (spread_hbm, spread),
                (caa_metric_hbm, caa_metric),
            ]
        )
    ]
    for load in loads:
        load.start()
    for load in loads[0:3]:
        load.wait()

    lane = lax.broadcasted_iota(jnp.int32, (rows, stream), 1)
    row = lax.broadcasted_iota(jnp.int32, (rows, stream), 0)
    slot_lanes = cap * block_nodes
    groups = stream // slot_lanes
    slot_of_lane = lax.rem(lane, slot_lanes) // block_nodes
    slot_of_row = lax.rem(row, slot_lanes) // block_nodes
    node_of_lane = lax.rem(lane, block_nodes)
    same_node = lax.rem(row, block_nodes) == node_of_lane
    one_lane = lane[0:1]
    block_of_lane = one_lane // block_nodes
    lead = jnp.zeros((1, stream), jnp.int32)
    trail = jnp.zeros((1, stream), jnp.int32)
    part = jnp.zeros((1, stream), jnp.int32)
    for j in range(stream // block_nodes):
        here = block_of_lane == j
        lead = jnp.where(here, refs[0, j] * cap + refs[1, j], lead)
        trail = jnp.where(here, refs[2, j] * cap + refs[3, j], trail)
        part = jnp.where(here, offsets[j], part)
    trail_weight = part.astype(F32) / 8.0
    lead_weight = 1.0 - trail_weight
    for d in range(n_gx):
        code = slot_of_row + d * cap
        weight = jnp.where(code == lead, lead_weight, 0.0) + jnp.where(code == trail, trail_weight, 0.0)
        weights[d * stream : (d + 1) * stream, :] = jnp.where(same_node, weight, 0.0).astype(BF16)
        taken = jnp.zeros((1, stream), jnp.int32)
        for c in range(cap):
            taken = jnp.where(slot_of_lane[0:1] == c, send_list[slab, d, c], taken)
        wanted = taken * block_nodes + node_of_lane[0:1]
        chooser[:, d * stream : (d + 1) * stream] = jnp.where(row == wanted, 1.0, 0.0).astype(BF16)

    def pair(sems, k, first, send, recv, devices):
        return [
            pltpu.make_async_remote_copy(
                src_ref=send.at[k, way], dst_ref=recv.at[k, way],
                send_sem=sems.at[k, first + way, 0], recv_sem=sems.at[k, first + way, 1],
                device_id=devices[way], device_id_type=MESH,
            )
            for way in range(2)
        ]

    def les_copies(k):
        copies = pair(les_sems, k, 0, les_az_send, les_az_recv, (above_id, below_id))
        return copies + pair(les_sems, k, 2, les_st_send, les_st_recv, (down_id, up_id))

    def caa_copies(k, ways=(0, 1)):
        copies = pair(caa_sems, k, 0, caa_az_send, caa_az_recv, (above_id, below_id))
        return [copies[way] for way in ways]

    def margin_copies(i):
        return [
            pltpu.make_async_remote_copy(
                src_ref=margin_send.at[i], dst_ref=margin_recv.at[i, way],
                send_sem=margin_sems.at[i, way, 0], recv_sem=margin_sems.at[i, way, 1],
                device_id=(down_id, up_id)[way], device_id_type=MESH,
            )
            for way in range(2)
        ]

    width = 2 * margin_nodes
    group = lane // width

    def send_margin(i, fields, first):
        packed = jnp.zeros((rows, stream), F32)
        for c, field in enumerate(fields, first):
            packed = jnp.where(group == c, pltpu.roll(field, width * c + margin_nodes, 1), packed)
        margin_send[i] = packed.astype(BF16)
        for copy in margin_copies(i):
            copy.start()

    def take_margin(i):
        for copy in margin_copies(i):
            copy.wait_recv()
        before = jnp.where(slab > 0, margin_recv[i, 0].astype(F32), 0.0)
        after = jnp.where(slab < slabs - 1, margin_recv[i, 1].astype(F32), 0.0)
        return jnp.where(lax.rem(lane, width) < margin_nodes, before, after)

    def swap_azimuth(value):
        at = lax.broadcasted_iota(jnp.int32, value.shape, 1) // width
        return jnp.where(lax.rem(at, 2) == 0, pltpu.roll(value, 2 * width, 1), 0.0)

    def swap_radial(value):
        return jnp.where(
            group == 0, pltpu.roll(value, width, 1), jnp.where(group == 3, pltpu.roll(value, 3 * width, 1), 0.0)
        )

    def lamb_copy(k, d):
        return pltpu.make_async_remote_copy(
            src_ref=lamb_send.at[k, d], dst_ref=lamb_recv.at[k, gx],
            send_sem=lamb_send_sem.at[k, d], recv_sem=lamb_recv_sem.at[k, gx],
            device_id={"sec": sec, "gx": d, "az": az}, device_id_type=MESH,
        )

    def lamb_arrival(k, d):
        return pltpu.make_async_remote_copy(
            src_ref=lamb_send.at[k, d], dst_ref=lamb_recv.at[k, d],
            send_sem=lamb_send_sem.at[k, d], recv_sem=lamb_recv_sem.at[k, d],
            device_id={"sec": sec, "gx": d, "az": az}, device_id_type=MESH,
        )

    radial_table = line_matrix(radial)

    def radial_apply(field):
        layers = [field[i * sector : (i + 1) * sector] for i in range(radial)]
        result = []
        for o in range(radial):
            terms = [float(radial_table[o, i]) * layers[i] for i in range(radial) if abs(radial_table[o, i]) > 1e-9]
            result.append(sum(terms[1:], terms[0]))
        return jnp.concatenate(result, axis=0)

    def ghosts(recv, k):
        before = jnp.where(slab > 0, recv[k, 0], 0.0)
        after = jnp.where(slab < slabs - 1, recv[k, 1], 0.0)
        return before, after

    def pieces(value, count):
        return [value[:, i * stream : (i + 1) * stream] for i in range(count)]

    for load in loads[3:]:
        load.wait()
    pl.semaphore_wait(barrier, 4 + len(partners))

    for k in range(LES_STEPS):
        u_ref = les_in if k == 0 else les_out
        for c in range(3):
            les_az_send[k, 0, c * radial : (c + 1) * radial] = u_ref[c, pl.ds(sector - 1, radial, stride=sector), :]
            les_az_send[k, 1, c * radial : (c + 1) * radial] = u_ref[c, pl.ds(0, radial, stride=sector), :]
        copies = les_copies(k)
        copies[0].start()
        copies[1].start()
        u = [u_ref[c] for c in range(3)]
        edges = pick_edges(wide(les_pick, 16), u)
        les_st_send[k, 0] = edges[8:16]
        les_st_send[k, 1] = edges[0:8]
        copies[2].start()
        copies[3].start()
        if k == 0:
            send_margin(0, [caa_metric[c] for c in range(3)], 0)
            send_margin(1, [caa_out[c] for c in range(4)], 0)

        stacked = [u + [u[j] * u[i] for i in range(3)] for j in range(3)]
        along = right_apply(stacked[0], stream_mat[...])
        along = [along[i * rows : (i + 1) * rows] for i in range(6)]
        around = pieces(left_apply(wide(azimuth_mat, rows), stacked[1]), 6)
        across = [radial_apply(field) for field in stacked[2]]

        for copy in copies:
            copy.wait_recv()
        before, after = ghosts(les_st_recv, k)
        third = lax.broadcasted_iota(jnp.int32, before.shape, 0) >= 3
        before = before * jnp.where(third, before[0:1], 1.0)
        after = after * jnp.where(third, after[0:1], 1.0)
        fix = pieces(stream_fix(jnp.concatenate([before, after], axis=0), wide(stream_ghost, 32)), 6)
        along = [a + b for a, b in zip(along, fix)]
        rim = []
        for c in range(3):
            rim.append([les_az_recv[k, way, c * radial : (c + 1) * radial] for way in range(2)])
        rim = rim + [[rim[1][way] * rim[c][way] for way in range(2)] for c in range(3)]
        rim = jnp.concatenate([jnp.concatenate(pair, axis=0) for pair in rim], axis=1)
        fix = pieces(azimuth_fix(azimuth_ghost[...], rim), 6)
        around = [a + b for a, b in zip(around, fix)]
        slopes = [
            [les_metric[0] * along[i] for i in range(3)],
            [les_metric[1] * around[i] for i in range(3)],
            [les_metric[2] * across[i] for i in range(3)],
        ]
        first = slopes[1][2] - slopes[2][1]
        second = slopes[2][0] - slopes[0][2]
        third = slopes[0][1] - slopes[1][0]
        lamb = jnp.concatenate(
            [
                second * u[2] - third * u[1],
                third * u[0] - first * u[2],
                first * u[1] - second * u[0],
            ],
            axis=0,
        ).astype(BF16)
        chosen = product(lamb, chooser[...])
        depth = 3 * rows // groups
        group_lane = lax.broadcasted_iota(jnp.int32, (depth, stream), 1) // slot_lanes
        for d in range(n_gx):
            mine = chosen[:, d * stream : (d + 1) * stream]
            packed = mine[0:depth]
            for g in range(1, groups):
                packed = jnp.where(group_lane == g, mine[g * depth : (g + 1) * depth], packed)
            lamb_send[k, d] = packed.astype(BF16)
        for d in partners:
            lamb_copy(k, d).start()
        lamb_recv[k, gx] = lamb_send[k, gx]

        for i in range(3):
            change = les_metric[0] * along[3 + i] + u[0] * slopes[0][i]
            change += les_metric[1] * around[3 + i] + u[1] * slopes[1][i]
            change += les_metric[2] * across[3 + i] + u[2] * slopes[2][i]
            les_out[i] = u[i] - (0.5 * les_step) * change

    rings = (pl.ds(sector - 1, radial, stride=sector), pl.ds(0, radial, stride=sector))

    def send_rows(k, way, p, v, m):
        caa_az_send[k, way, 0:radial] = p
        caa_az_send[k, way, radial : 2 * radial] = v
        caa_az_send[k, way, 2 * radial : 3 * radial] = swap_azimuth(m)
        caa_copies(k)[way].start()

    def substep(k, fresh, last):
        w = [caa_out[c] for c in range(4)]
        m = margin[...]
        high, low = split(jnp.concatenate(w, axis=0))
        m_high = m.astype(BF16)
        both = product(
            jnp.concatenate([high, low, high], axis=1), jnp.concatenate([stream_mat[...], joint[...]], axis=1)
        )
        fix = pieces(product(m_high, wide(inner, rows)), 4)
        along = [caa_metric[0] * (both[c * rows : (c + 1) * rows, 0:stream] + fix[c]) for c in range(4)]
        edges = [both[c * rows : (c + 1) * rows, stream : 2 * stream] for c in range(4)]
        partner = jnp.where(group == 0, edges[1], jnp.where(group == 1, edges[0], 0.0))
        own = jnp.where(group < 2, jnp.where(group == 0, edges[0], edges[1]), jnp.where(group == 2, edges[2], edges[3]))
        m_along = product(jnp.concatenate([m_high, m_high], axis=1), margin_mat[...]) + (mach_number * own + partner)
        w_high = [high[c * rows : (c + 1) * rows] for c in range(4)]
        w_low = [low[c * rows : (c + 1) * rows] for c in range(4)]
        table = wide(azimuth_mat, rows)
        top = jnp.concatenate([w_high[0], w_high[2]], axis=1)
        under = jnp.concatenate([w_low[0], w_low[2]], axis=1)
        around = pieces(product(table, jnp.concatenate([top, under, top], axis=0)), 2)
        swapped = swap_azimuth(m).astype(BF16)
        around.append(product(table[:, rows : 3 * rows], jnp.concatenate([swapped, swapped], axis=0)))
        across = [radial_apply(field) for field in (w[0], w[3], swap_radial(m))]
        rates = [
            mach_number * along[0] + along[1] + caa_metric[1] * around[1] + caa_metric[2] * across[1],
            mach_number * along[1] + along[0] - source[0:rows],
            mach_number * along[2] + caa_metric[1] * around[0] - source[rows : 2 * rows],
            mach_number * along[3] + caa_metric[2] * across[0] - source[2 * rows : 3 * rows],
        ]
        for c in range(4):
            caa_out[c] = w[c] - caa_step * rates[c]
        if fresh is not None:
            margin_source[...] = take_margin(fresh)
        rate = margin_metric[0] * m_along + margin_metric[1] * around[2] + margin_metric[2] * across[2]
        margin[...] = m - caa_step * (rate - margin_source[...])

        copies = caa_copies(k)
        for way in range(2):
            copies[way].wait_recv()
            ring = rings[1 - way]
            scale = (3.0 * caa_step) * (1.0 - 2.0 * way)
            halo = [caa_az_recv[k, way, c * radial : (c + 1) * radial] for c in range(3)]
            p = caa_out[0, ring, :] + scale * caa_metric[1, ring, :] * halo[1]
            v = caa_out[2, ring, :] + scale * caa_metric[1, ring, :] * halo[0]
            edge = margin[ring, :] + scale * margin_metric[1, ring, :] * halo[2]
            caa_out[0, ring, :] = p
            caa_out[2, ring, :] = v
            margin[ring, :] = edge
            if not last:
                send_rows(k + 1, 1 - way, p, v, edge)

    def later_substep(k, carry):
        substep(k, None, False)
        return carry

    for k in range(LES_STEPS):
        if k > 0:
            send_margin(1 + 2 * k, [caa_out[c] for c in range(4)], 0)
        for d in partners:
            lamb_arrival(k, d).wait_recv()
        depth = 3 * rows // groups
        group_lane = lax.broadcasted_iota(jnp.int32, (depth, stream), 1) // slot_lanes
        for g in range(groups):
            got = [
                jnp.where(group_lane == g, lamb_recv[k, d].astype(F32), 0.0).astype(BF16) for d in range(n_gx)
            ]
            source[g * depth : (g + 1) * depth, :] = product(jnp.concatenate(got, axis=1), weights[...])
        send_margin(2 + 2 * k, [source[c * rows : (c + 1) * rows, :] for c in range(3)], 1)
        if k == 0:
            table = wide(spread, rows)
            spread_metric = pieces(product(take_margin(0).astype(BF16), table), 3)
            for c in range(3):
                margin_metric[c] = spread_metric[c]
        margin[...] = take_margin(1 + 2 * k)
        begin = k * CAA_SUB
        for way in range(2):
            ring = rings[way]
            send_rows(begin, way, caa_out[0, ring, :], caa_out[2, ring, :], margin[ring, :])
        substep(begin, 2 + 2 * k, False)
        lax.fori_loop(begin + 1, begin + CAA_SUB - 1, later_substep, 0)
        substep(begin + CAA_SUB - 1, None, True)

    def drain_caa(k, carry):
        for copy in caa_copies(k):
            copy.wait_send()
        return carry

    lax.fori_loop(0, LES_STEPS * CAA_SUB, drain_caa, 0)
    for i in range(1 + 2 * LES_STEPS):
        for copy in margin_copies(i):
            copy.wait_send()
    for k in range(LES_STEPS):
        for copy in les_copies(k):
            copy.wait_send()
        for d in partners:
            lamb_copy(k, d).wait_send()


def hand_over(les_from, caa_from, les_to, caa_to, les_held, caa_held, sems):
    chains = ((les_from, les_held, les_to), (caa_from, caa_held, caa_to))
    loads = [pltpu.make_async_copy(a, b, sems.at[i]) for i, (a, b, _) in enumerate(chains)]
    stores = [pltpu.make_async_copy(b, c, sems.at[2 + i]) for i, (_, b, c) in enumerate(chains)]
    for load in loads:
        load.start()
    for load, store in zip(loads, stores):
        load.wait()
        store.start()
    for store in stores:
        store.wait()


def solution(mesh):
    n_sec, n_gx, n_az = mesh.shape["sec"], mesh.shape["gx"], mesh.shape["az"]

    def body(les_velocity, les_metric, caa_state, caa_metric, intersection_refs, offsets, send_list):
        radial, sector, stream = les_velocity.shape[1:]
        cap = send_list.shape[2]
        rows = radial * sector
        sizes = (n_sec, n_gx, n_az, radial, sector, stream, cap)
        consts = [jnp.asarray(t) for t in tables(radial, sector, stream)]
        flat = lambda x: x.reshape(x.shape[0], rows, stream)
        substeps = LES_STEPS * CAA_SUB
        depth = 3 * rows // (stream // (cap * block_nodes))
        vmem = pl.BlockSpec(memory_space=pltpu.VMEM)
        hbm = pl.BlockSpec(memory_space=pltpu.HBM)
        les_out, caa_out = pl.pallas_call(
            functools.partial(kernel, sizes),
            out_shape=(
                jax.ShapeDtypeStruct((3, rows, stream), F32),
                jax.ShapeDtypeStruct((4, rows, stream), F32),
            ),
            in_specs=[hbm] * (7 + len(consts)),
            out_specs=(vmem, vmem),
            scratch_shapes=[
                pltpu.VMEM((3, rows, stream), F32),
                pltpu.VMEM((3, rows, stream), F32),
                pltpu.VMEM((3, rows, stream), F32),
                pltpu.SMEM(intersection_refs.shape[::-1], jnp.int32),
                pltpu.SMEM(offsets.shape, jnp.int32),
                pltpu.SMEM(send_list.shape, jnp.int32),
            ]
            + [pltpu.VMEM(t.shape, BF16) for t in consts]
            + [
                pltpu.SemaphoreType.DMA((7 + len(consts),)),
                pltpu.VMEM((3 * rows, stream), F32),
                pltpu.VMEM((n_gx * stream, stream), BF16),
                pltpu.VMEM((rows, n_gx * stream), BF16),
                pltpu.VMEM((LES_STEPS, 2, 3 * radial, stream), F32),
                pltpu.VMEM((LES_STEPS, 2, 3 * radial, stream), F32),
                pltpu.VMEM((LES_STEPS, 2, 8, rows), F32),
                pltpu.VMEM((LES_STEPS, 2, 8, rows), F32),
                pltpu.VMEM((substeps, 2, 3 * radial, stream), F32),
                pltpu.VMEM((substeps, 2, 3 * radial, stream), F32),
                pltpu.VMEM((1 + 2 * LES_STEPS, rows, stream), BF16),
                pltpu.VMEM((1 + 2 * LES_STEPS, 2, rows, stream), BF16),
                pltpu.VMEM((rows, stream), F32),
                pltpu.VMEM((3, rows, stream), F32),
                pltpu.VMEM((rows, stream), F32),
                pltpu.VMEM((LES_STEPS, n_gx, depth, stream), BF16),
                pltpu.VMEM((LES_STEPS, n_gx, depth, stream), BF16),
                pltpu.SemaphoreType.DMA((LES_STEPS, 4, 2)),
                pltpu.SemaphoreType.DMA((substeps, 2, 2)),
                pltpu.SemaphoreType.DMA((1 + 2 * LES_STEPS, 2, 2)),
                pltpu.SemaphoreType.DMA((LES_STEPS, n_gx)),
                pltpu.SemaphoreType.DMA((LES_STEPS, n_gx)),
            ],
            compiler_params=pltpu.CompilerParams(
                collective_id=0, has_side_effects=True, vmem_limit_bytes=63 * 2**20
            ),
        )(
            flat(les_velocity), flat(les_metric), flat(caa_state), flat(caa_metric),
            intersection_refs.T, offsets, send_list, *consts,
        )
        shapes = [(3, rows, stream), (4, rows, stream)]
        les_out, caa_out = pl.pallas_call(
            hand_over,
            out_shape=tuple(jax.ShapeDtypeStruct(shape, F32) for shape in shapes),
            in_specs=[hbm] * 2,
            out_specs=(hbm, hbm),
            scratch_shapes=[pltpu.VMEM(shape, F32) for shape in shapes] + [pltpu.SemaphoreType.DMA((4,))],
            compiler_params=pltpu.CompilerParams(vmem_limit_bytes=63 * 2**20),
        )(les_out, caa_out)
        return les_out.reshape(les_velocity.shape), caa_out.reshape(caa_state.shape)

    in_specs = (
        P(None, None, "az", ("sec", "gx")),
        P(None, None, "az", ("sec", "gx")),
        P(None, None, "az", ("sec", "gx")),
        P(None, None, "az", ("sec", "gx")),
        P(("sec", "gx"), None),
        P(("sec", "gx")),
        P(),
    )
    out_specs = (P(None, None, "az", ("sec", "gx")), P(None, None, "az", ("sec", "gx")))
    return jax.shard_map(body, mesh=mesh, in_specs=in_specs, out_specs=out_specs, check_vma=False)
```
